512 devices in a mesh: dp: 32 (over x_hi, y, core), fsdp: 16 (over z, x_lo).
Axes of the slice: x: 4 (x_hi: 2, x_lo: 2; x = x_hi * 2 + x_lo), y: 8, z: 8, core: 2. Of those that a mesh axis runs over, the one named last changes fastest.
Arguments:
- latents: bfloat16 [1024, 96, 1024], P(('dp', 'fsdp')), may hold values from -6 to 6
- targets: bfloat16 [1024, 96, 1024], P(('dp', 'fsdp')), may hold values from -6 to 6
- rewards: float32 [1024], P(('dp', 'fsdp')), may hold values from 0.2 to 5
- time_steps: int32 [1024], P(('dp', 'fsdp')), may hold values from 0 to 999
- time_table: float32 [1000, 96], replicated, may hold values from -6 to 6
- norm_gain: float32 [96], replicated, may hold values from 0.5 to 1.5
- norm_bias: float32 [96], replicated, may hold values from -3 to 3
- expert_weights: bfloat16 [8, 96, 2592], P(None, 'fsdp'), may hold values from -0.125 to 0.125
- lane_experts: int32 [32, 2], P('dp'), may hold values from 0 to 7, all different within a row
- lane_counts: int32 [32, 2], P('dp'), may hold values from 1 to 31, as said below
Outputs:
- grad_weight: float32 [8, 96, 2592], P(None, 'fsdp')
- grad_input: bfloat16 [1024, 96, 1024], P(('dp', 'fsdp'))
The draws below stay inside these ranges and needn't reach their ends.
Inputs may be any that keep to these rules, and one draw needn't show every extreme that they name: `lane_experts`: the two experts of a lane differ, and every expert belongs to some lane. `lane_counts`: both counts of a lane are at least 1 and add up to at most 32; some lane is full in every draw. A lane's slots hold its first expert's samples, then its second's, then empty slots.
All inputs are finite; a program needn't handle non-finite values.
Results may differ from the reference program's by a relative error of at most 0.015.
Values may be sent and summed in bfloat16 or wider, within the bound.
A program may use at most 64 MiB of HBM per device.

```python
import math
import jax
import jax.numpy as jnp
from jax import lax

C = 96
EXPERTS = 8
TSTEPS = 1000
GROUPS = 32
TAPS = 27
SIDE = 16
DEPTH = 4
CELLS = 1024
LANES = 32
LANE_SLOTS = 32
TOTAL = 1024


def draw_lane_counts(key, part):
    key = jax.random.fold_in(key, 11)
    key_total, key_split, key_full = jax.random.split(key, 3)
    lowest = max(2, LANE_SLOTS // 3)
    totals = jax.random.randint(key_total, (LANES,), lowest, LANE_SLOTS + 1)
    full_lane = jax.random.randint(key_full, (), 0, LANES)
    is_full = jnp.arange(LANES) == full_lane
    totals = jnp.where(is_full, LANE_SLOTS, totals).astype(jnp.int32)
    first = jax.random.randint(key_split, (LANES,), 1, totals).astype(jnp.int32)
    first = jnp.where(is_full, LANE_SLOTS - 1, first).astype(jnp.int32)
    second = totals - first
    return jnp.stack([first, second], axis=1).astype(jnp.int32)


def plant(array, stream_key, low, high):
    spot = [jax.random.randint(jax.random.fold_in(stream_key, axis), (), 0, length) for axis, length in enumerate(array.shape)]
    widest = array.shape.index(max(array.shape))
    next_to = spot[:widest] + [(spot[widest] + 1) % array.shape[widest]] + spot[widest + 1:]
    return array.at[tuple(spot)].set(low).at[tuple(next_to)].set(high)


def steps_of(own_key, shape, shards, smallest, top_value):
    factor_of, own = 1.0, jax.random.fold_in(own_key, 6)
    for axis_at, blocks in shards:
        draws = jnp.exp(jax.random.uniform(jax.random.fold_in(own, axis_at), (blocks,), jnp.float32, smallest / len(shards), top_value / len(shards)))
        factor_of = factor_of * jnp.repeat(draws, shape[axis_at] // blocks).reshape([-1 if axis == axis_at else 1 for axis in range(len(shape))])
    return factor_of


def different_ones(stream_key, rows, count, top, lift):
    sequence = jax.random.permutation(jax.random.fold_in(stream_key, 1), count)
    boost = sequence
    for power in range(3):
        boost = boost * boost // count
    boost = boost * lift // count
    chance = jax.random.randint(jax.random.fold_in(stream_key, 2), (rows, count), 0, 4096) + boost
    holders = jax.random.permutation(jax.random.fold_in(stream_key, 3), rows)[jnp.arange(count) % rows]
    chance = jnp.where(jnp.arange(rows)[:, None] == holders[None, :], 1 << 14, chance)
    merit = chance * count + jnp.arange(count)
    return lax.top_k(merit.astype(jnp.int32), top)[1].astype(jnp.int32)


def bell_draw(key, extent, scale, bound, cuts=(), kind=jnp.bfloat16):
    factor_of = steps_of(key, extent, cuts, -0.22, 0.18) if cuts else 1.0
    array = jax.random.normal(key, extent, jnp.float32) * scale * factor_of
    return jnp.minimum(jnp.maximum(array, -bound), bound).astype(kind)


def setup_inputs(seed: int = 0) -> dict:
    key_of = jax.random.split(jax.random.key(seed), 11)
    return {
        "latents": bell_draw(key_of[0], (TOTAL, C, CELLS), 1.0, 6.0, ((0, 512),)),
        "targets": bell_draw(key_of[1], (TOTAL, C, CELLS), 1.0, 6.0, ((0, 512),)),
        "rewards": jnp.clip(jnp.exp(math.log(5.0) - 3.218876 * jax.random.uniform(key_of[2], (TOTAL,), jnp.float32) ** steps_of(key_of[2], (TOTAL,), ((0, 512),), -0.2, 0.2)), 0.2, 5.0),
        "time_steps": plant(jax.random.randint(key_of[3], (TOTAL,), 0, TSTEPS), jax.random.fold_in(key_of[3], 1), 0, TSTEPS - 1).astype(jnp.int32),
        "time_table": bell_draw(key_of[4], (TSTEPS, C), 1.0, 6.0, (), jnp.float32),
        "norm_gain": jnp.clip(1.0 + 0.1 * jax.random.normal(key_of[5], (C,), jnp.float32), 0.5, 1.5),
        "norm_bias": bell_draw(key_of[6], (C,), 0.5, 3.0, (), jnp.float32),
        "expert_weights": bell_draw(key_of[7], (EXPERTS, C, TAPS * C), (TAPS * C) ** -0.5, 0.125, ((1, 16),)),
        "lane_experts": different_ones(key_of[8], LANES, EXPERTS, 2, 0),
        "lane_counts": draw_lane_counts(jax.random.fold_in(key_of[10], 71), 0),
    }


EPSILON = 1e-05

def tap_list():
    result = []
    for step_x in (-1, 0, 1):
        for step_y in (-1, 0, 1):
            for step_z in (-1, 0, 1):
                result.append((step_x, step_y, step_z))
    return result

def shift_cells(values, step_x, step_y, step_z):
    plane = SIDE * SIDE
    total = DEPTH * plane
    position = jnp.arange(total, dtype=jnp.int32)
    depth_at = position // plane
    row_at = position // SIDE % SIDE
    column_at = position % SIDE
    inside = (depth_at + step_x >= 0) & (depth_at + step_x < DEPTH) & (row_at + step_y >= 0) & (row_at + step_y < SIDE) & (column_at + step_z >= 0) & (column_at + step_z < SIDE)
    offset = step_x * plane + step_y * SIDE + step_z
    reach = plane + SIDE + 1
    widths = [(0, 0)] * (values.ndim - 1) + [(reach, reach)]
    padded = jnp.pad(values, widths)
    moved_cells = lax.slice_in_dim(padded, reach + offset, reach + offset + total, axis=values.ndim - 1)
    return jnp.where(inside, moved_cells, jnp.zeros_like(moved_cells))

def unfold_taps(activ_rows):
    pieces = []
    for offset in tap_list():
        pieces.append(shift_cells(activ_rows, offset[0], offset[1], offset[2]))
    return jnp.concatenate(pieces, axis=0)

def fold_back(products):
    channels = products.shape[0] // TAPS
    total = jnp.zeros((channels, products.shape[1]), jnp.float32)
    for tap_index, offset in enumerate(tap_list()):
        block = products[tap_index * channels:(tap_index + 1) * channels]
        total = total + shift_cells(block, -offset[0], -offset[1], -offset[2])
    return total

def norm_act(field, norm_gain, norm_bias):
    lead = field.shape[:-2]
    channels = field.shape[-2]
    grouped = field.reshape(lead + (GROUPS, channels // GROUPS * field.shape[-1]))
    centre = lax.optimization_barrier(jnp.mean(grouped, axis=-1, keepdims=True))
    spread = lax.optimization_barrier(jnp.mean(jnp.square(grouped - centre), axis=-1, keepdims=True))
    normed = ((grouped - centre) * lax.rsqrt(spread + EPSILON)).reshape(field.shape)
    return jax.nn.silu(normed * norm_gain[:, None] + norm_bias[:, None])

def reference(latents, targets, rewards, time_steps, time_table, norm_gain, norm_bias, expert_weights, lane_experts, lane_counts):
    slot_ids = jnp.arange(TOTAL, dtype=jnp.int32)
    lane_of = slot_ids // LANE_SLOTS
    place = slot_ids % LANE_SLOTS
    counts = lane_counts[lane_of]
    pair = lane_experts[lane_of]
    in_first = place < counts[:, 0]
    in_second = (place >= counts[:, 0]) & (place < counts[:, 0] + counts[:, 1])
    expert_of = jnp.where(in_second, pair[:, 1], pair[:, 0]).astype(jnp.int32)
    live = jnp.where(in_first | in_second, 1.0, 0.0).astype(jnp.float32)
    slot_weight = rewards * live
    embedded = time_table[time_steps]

    def visit(table, inputs):
        latent, target, weight, embed, expert = inputs
        weights = lax.dynamic_index_in_dim(expert_weights, expert, 0, keepdims=False)
        start = latent.astype(jnp.float32) + embed[:, None]
        activ, back_fn = jax.vjp(lambda field: norm_act(field, norm_gain, norm_bias), start)
        columns = unfold_taps(activ.astype(jnp.bfloat16))
        mixed = jnp.dot(weights, columns, preferred_element_type=jnp.float32)
        upstream = weight * (latent.astype(jnp.float32) + mixed - target.astype(jnp.float32))
        upstream_b = upstream.astype(jnp.bfloat16)
        grad_w = lax.dot_general(upstream_b, columns, (((1,), (1,)), ((), ())), preferred_element_type=jnp.float32) / CELLS
        table = table.at[expert].add(grad_w)
        products = lax.dot_general(weights, upstream_b, (((0,), (0,)), ((), ())), preferred_element_type=jnp.float32)
        grad_act = fold_back(products)
        grad_start = back_fn(grad_act)[0]
        grad_input = (upstream + grad_start).astype(jnp.bfloat16)
        return (table, grad_input)
    empty = jnp.zeros((EXPERTS, C, TAPS * C), jnp.float32)
    table, grad_input = lax.scan(visit, empty, (latents, targets, slot_weight, embedded, expert_of))
    return (table, grad_input)
```

```python
import jax
import jax.numpy as jnp
from jax import lax
from jax.experimental import pallas as pl
from jax.experimental.pallas import tpu as pltpu
from jax.sharding import PartitionSpec as P

GROUPS = 32
SIDE = 16
DEPTH = 4


EPSILON = 1e-05

MESH = pl.DeviceIdType.MESH
ROWS = 16
WIDE = 2688
TILES = 21
VMEM = pl.BlockSpec(memory_space=pltpu.VMEM)


def rcopy(src, dst, sems, at, device_id):
    return pltpu.make_async_remote_copy(
        src_ref=src,
        dst_ref=dst,
        send_sem=sems[0].at[at],
        recv_sem=sems[1].at[at],
        device_id=device_id,
        device_id_type=MESH,
    )


def ring_place():
    f = lax.axis_index("fsdp")
    z = f // 2
    x = f % 2
    nbr = z * 2 + 1 - x
    up = lax.rem(z + 1, 8) * 2 + x
    down = lax.rem(z + 7, 8) * 2 + x
    return f, z, x, nbr, up, down


def gather_kernel(shard_ref, out_ref, send_sem, recv_sem):
    f, z, x, nbr, up, down = ring_place()
    sems = (send_sem, recv_sem)
    barrier = pltpu.get_barrier_semaphore()
    for other in (nbr, up, down):
        pl.semaphore_signal(barrier, inc=1, device_id={"fsdp": other}, device_id_type=MESH)
    pl.semaphore_wait(barrier, 3)
    out_ref[f] = shard_ref[...]
    hops = {(0, 0): 4, (0, 1): 3, (1, 0): 3, (1, 1): 4}
    base = {}
    count = 1
    for key, n in hops.items():
        base[key] = count
        count += n

    def make(key, h):
        col, direction = key
        zz = lax.rem(z + 8 - h, 8) if direction == 0 else lax.rem(z + h, 8)
        item = zz * 2 + (x if col == 0 else 1 - x)
        return rcopy(
            out_ref.at[item], out_ref.at[item], sems, base[key] + h,
            {"fsdp": up if direction == 0 else down},
        )

    copies = {}
    swap = rcopy(shard_ref, out_ref.at[f], sems, 0, {"fsdp": nbr})
    swap.start()
    for key in ((0, 0), (0, 1)):
        copies[key] = [make(key, 0)]
        copies[key][0].start()
    swap.wait_recv()
    for key in ((1, 0), (1, 1)):
        copies[key] = [make(key, 0)]
        copies[key][0].start()
    for h in range(1, 5):
        for key, n in hops.items():
            if h <= n:
                copies[key][h - 1].wait_recv()
            if h < n:
                copies[key].append(make(key, h))
                copies[key][h].start()
    swap.wait_send()
    for key in hops:
        for copy in copies[key]:
            copy.wait_send()


def gather(shard):
    return pl.pallas_call(
        gather_kernel,
        out_shape=jax.ShapeDtypeStruct((16, ROWS, WIDE), jnp.bfloat16),
        in_specs=[VMEM],
        out_specs=VMEM,
        scratch_shapes=[pltpu.SemaphoreType.DMA((15,)), pltpu.SemaphoreType.DMA((15,))],
        compiler_params=pltpu.CompilerParams(
            collective_id=0, has_side_effects=True, vmem_limit_bytes=40 * 2**20
        ),
    )(shard)


def reduce_kernel(
    part_ref, place_ref, out_ref, held, stage, total, swap_out, swap_in, table, core_in, half,
    chunk_in, full, ring_s, ring_r, dp_s, dp_r,
):
    f, z, x, nbr, up, down = ring_place()
    ring = (ring_s, ring_r)
    lanes = (dp_s, dp_r)
    d = lax.axis_index("dp")
    core = d % 2
    chip = d // 2
    twin = chip * 2 + 1 - core
    peers = [lax.rem(chip + i, 16) for i in range(1, 16)]
    barrier = pltpu.get_barrier_semaphore()
    for other in (nbr, up, down):
        pl.semaphore_signal(barrier, inc=1, device_id={"fsdp": other}, device_id_type=MESH)
    pl.semaphore_signal(barrier, inc=1, device_id={"dp": twin}, device_id_type=MESH)
    for peer in peers:
        pl.semaphore_signal(
            barrier, inc=1, device_id={"dp": peer * 2 + core}, device_id_type=MESH
        )
    pl.semaphore_wait(barrier, 19)

    f32 = jnp.float32
    hops = {(0, 0): 4, (0, 1): 3, (1, 0): 3, (1, 1): 4}
    base = {}
    count = 0
    for key, n in hops.items():
        base[key] = count
        count += n
    copies = {}
    for h in range(4):
        for key, n in hops.items():
            if h >= n:
                continue
            col, direction = key
            away = n - h
            zz = lax.rem(z + away, 8) if direction == 0 else lax.rem(z + 8 - away, 8)
            at = base[key] + h
            if h == 0:
                src = part_ref.at[zz * 2 + col]
                copies[key] = []
            else:
                copies[key][h - 1].wait_recv()
                stage[at] = (
                    held[at - 1].astype(f32) + part_ref[zz * 2 + col].astype(f32)
                ).astype(jnp.bfloat16)
                src = stage.at[at]
            copy = rcopy(src, held.at[at], ring, at, {"fsdp": up if direction == 0 else down})
            copy.start()
            copies[key].append(copy)
    for col in (0, 1):
        for direction in (0, 1):
            key = (col, direction)
            copies[key][-1].wait_recv()
        value = (
            part_ref[z * 2 + col].astype(f32)
            + held[base[(col, 0)] + hops[(col, 0)] - 1].astype(f32)
            + held[base[(col, 1)] + hops[(col, 1)] - 1].astype(f32)
        )
        total[col] = value
        swap_out[col] = value.astype(jnp.bfloat16)
    swap = rcopy(swap_out.at[1 - x], swap_in, ring, 14, {"fsdp": nbr})
    swap.start()
    swap.wait_recv()
    lane = (total[x] + swap_in[...].astype(f32)).astype(jnp.bfloat16)
    spread = jnp.dot(place_ref[...], lane, preferred_element_type=f32).astype(jnp.bfloat16)
    for row in range(3):
        for tile in range(TILES):
            table[row * TILES + tile] = spread[
                row * ROWS : (row + 1) * ROWS, tile * 128 : (tile + 1) * 128
            ]
    table[63] = jnp.zeros((ROWS, 128), jnp.bfloat16)

    mine = core * 32
    pair = rcopy(table.at[pl.ds(32 - mine, 32)], core_in, lanes, 30, {"dp": twin})
    pair.start()
    pair.wait_recv()
    half[...] = (table[pl.ds(mine, 32)].astype(f32) + core_in[...].astype(f32)).astype(
        jnp.bfloat16
    )
    scatters = []
    for i, peer in enumerate(peers):
        copy = rcopy(
            half.at[pl.ds(peer * 2, 2)], chunk_in.at[i], lanes, i, {"dp": peer * 2 + core}
        )
        copy.start()
        scatters.append(copy)
    acc = half[pl.ds(chip * 2, 2)].astype(f32)
    for i, copy in enumerate(scatters):
        copy.wait_recv()
        acc = acc + chunk_in[i].astype(f32)
    own = pl.ds(mine + chip * 2, 2)
    full[own] = acc.astype(jnp.bfloat16)
    gathers = []
    for i, peer in enumerate(peers):
        copy = rcopy(full.at[own], full.at[own], lanes, 15 + i, {"dp": peer * 2 + core})
        copy.start()
        gathers.append(copy)
    for copy in gathers:
        copy.wait_recv()
    both = pl.ds(mine, 32)
    last = rcopy(full.at[both], full.at[both], lanes, 31, {"dp": twin})
    last.start()
    last.wait_recv()
    for tile in range(TILES):
        block = jnp.concatenate(
            [full[row * TILES + tile].astype(f32) for row in range(3)], axis=0
        )
        wide = min(128, 2592 - tile * 128)
        for expert in range(8):
            out_ref[expert, :, tile * 128 : tile * 128 + wide] = block[
                expert * 6 : expert * 6 + 6, :wide
            ]
    for key in hops:
        for copy in copies[key]:
            copy.wait_send()
    swap.wait_send()
    pair.wait_send()
    last.wait_send()
    for copy in scatters + gathers:
        copy.wait_send()


def reduce_all(part, place):
    bf16 = jnp.bfloat16
    return pl.pallas_call(
        reduce_kernel,
        out_shape=jax.ShapeDtypeStruct((8, 6, 2592), jnp.float32),
        in_specs=[VMEM, VMEM],
        out_specs=VMEM,
        scratch_shapes=[
            pltpu.VMEM((14, ROWS, WIDE), bf16),
            pltpu.VMEM((14, ROWS, WIDE), bf16),
            pltpu.VMEM((2, ROWS, WIDE), jnp.float32),
            pltpu.VMEM((2, ROWS, WIDE), bf16),
            pltpu.VMEM((ROWS, WIDE), bf16),
            pltpu.VMEM((64, ROWS, 128), bf16),
            pltpu.VMEM((32, ROWS, 128), bf16),
            pltpu.VMEM((32, ROWS, 128), bf16),
            pltpu.VMEM((15, 2, ROWS, 128), bf16),
            pltpu.VMEM((64, ROWS, 128), bf16),
            pltpu.SemaphoreType.DMA((15,)),
            pltpu.SemaphoreType.DMA((15,)),
            pltpu.SemaphoreType.DMA((32,)),
            pltpu.SemaphoreType.DMA((32,)),
        ],
        compiler_params=pltpu.CompilerParams(
            collective_id=1, has_side_effects=True, vmem_limit_bytes=40 * 2**20
        ),
    )(part, place)


def place_matrix(pick):
    body = jnp.einsum("je,rq->erjq", pick, jnp.eye(6, dtype=jnp.float32)).reshape(48, 12)
    return jnp.pad(body, ((0, 0), (0, 4))).astype(jnp.bfloat16)


def tap_list():
    result = []
    for step_x in (-1, 0, 1):
        for step_y in (-1, 0, 1):
            for step_z in (-1, 0, 1):
                result.append((step_x, step_y, step_z))
    return result


def shift_cells(values, step_x, step_y, step_z):
    plane = SIDE * SIDE
    total = DEPTH * plane
    position = jnp.arange(total, dtype=jnp.int32)
    depth_at = position // plane
    row_at = position // SIDE % SIDE
    column_at = position % SIDE
    inside = (
        (depth_at + step_x >= 0)
        & (depth_at + step_x < DEPTH)
        & (row_at + step_y >= 0)
        & (row_at + step_y < SIDE)
        & (column_at + step_z >= 0)
        & (column_at + step_z < SIDE)
    )
    offset = step_x * plane + step_y * SIDE + step_z
    reach = plane + SIDE + 1
    widths = [(0, 0)] * (values.ndim - 1) + [(reach, reach)]
    padded = jnp.pad(values, widths)
    moved_cells = lax.slice_in_dim(
        padded, reach + offset, reach + offset + total, axis=values.ndim - 1
    )
    return jnp.where(inside, moved_cells, jnp.zeros_like(moved_cells))


def unfold_taps(activ_rows):
    pieces = []
    for offset in tap_list():
        pieces.append(shift_cells(activ_rows, offset[0], offset[1], offset[2]))
    return jnp.concatenate(pieces, axis=0)


def norm_act(field, norm_gain, norm_bias):
    lead = field.shape[:-2]
    channels = field.shape[-2]
    grouped = field.reshape(lead + (GROUPS, channels // GROUPS * field.shape[-1]))
    centre = jnp.mean(grouped, axis=-1, keepdims=True)
    spread = jnp.mean(jnp.square(grouped - centre), axis=-1, keepdims=True)
    normed = ((grouped - centre) * lax.rsqrt(spread + EPSILON)).reshape(field.shape)
    return jax.nn.silu(normed * norm_gain[:, None] + norm_bias[:, None])


def local(
    latents,
    targets,
    rewards,
    time_steps,
    time_table,
    norm_gain,
    norm_bias,
    expert_weights,
    lane_experts,
    lane_counts,
):
    slots = latents.shape[0]
    channels = latents.shape[1]
    experts_all = expert_weights.shape[0]
    offsets = tap_list()
    lane_pair = lane_experts[0]
    counts = lane_counts[0]
    place = lax.axis_index("fsdp") * slots + jnp.arange(slots, dtype=jnp.int32)
    in_first = place < counts[0]
    in_second = (place >= counts[0]) & (place < counts[0] + counts[1])
    member = jnp.stack([in_first, in_second], axis=1).astype(jnp.float32)
    which = jnp.where(in_second, 1, 0).astype(jnp.int32)
    slot_weight = rewards * jnp.sum(member, axis=1)
    pick = (lane_pair[:, None] == jnp.arange(experts_all, dtype=jnp.int32)[None, :]).astype(
        jnp.float32
    )
    lane_shards = jnp.einsum(
        "je,erk->jrk", pick.astype(jnp.bfloat16), expert_weights, preferred_element_type=jnp.float32
    ).astype(jnp.bfloat16)
    table_rows = time_table.shape[0]
    one_hot = (time_steps[:, None] == jnp.arange(table_rows, dtype=jnp.int32)[None, :]).astype(
        jnp.float32
    )
    embedded = jnp.dot(
        one_hot, time_table, precision=lax.Precision.HIGHEST, preferred_element_type=jnp.float32
    )
    starts = latents.astype(jnp.float32) + embedded[:, :, None]
    activ, back_fn = jax.vjp(lambda field: norm_act(field, norm_gain, norm_bias), starts)
    activ_b = activ.astype(jnp.bfloat16)
    columns = [unfold_taps(activ_b[slot_index]) for slot_index in range(slots)]
    holder = {}
    shard = jnp.pad(lane_shards.reshape(12, -1), ((0, 4), (0, WIDE - 2592)))
    piece = gather(shard)[:, :12, :2592].reshape(16, 2, 6, 2592).swapaxes(0, 1).reshape(2, 96, 2592)
    outputs = []
    for slot_index in range(slots):
        chosen = lax.dynamic_index_in_dim(piece, which[slot_index], 0, keepdims=False)
        outputs.append(jnp.dot(chosen, columns[slot_index], preferred_element_type=jnp.float32))
    mixed = jnp.stack(outputs, axis=0)
    upstream = slot_weight[:, None, None] * (
        latents.astype(jnp.float32) + mixed - targets.astype(jnp.float32)
    )
    upstream_b = upstream.astype(jnp.bfloat16)
    holder["upstream"] = upstream_b
    cells = latents.shape[2]
    pieces = []
    for weight_slot_index in range(slots):
        weight_rows_grad = upstream_b[weight_slot_index]
        pieces.append(
            lax.dot_general(
                weight_rows_grad,
                columns[weight_slot_index],
                (((1,), (1,)), ((), ())),
                preferred_element_type=jnp.float32,
            )
        )
    stacked = jnp.stack(pieces, axis=0) / cells
    sums = jnp.einsum("sj,srk->rjk", member, stacked, precision=lax.Precision.HIGHEST).astype(
        jnp.bfloat16
    )
    part = sums.reshape(16, 6, 2, 2592).swapaxes(1, 2).reshape(16, 12, 2592)
    part = jnp.pad(part, ((0, 0), (0, 4), (0, WIDE - 2592)))
    grad_weight = reduce_all(part, place_matrix(pick))
    add_upstream_b = holder["upstream"]
    updates = []
    for slot_index in range(slots):
        chosen = lax.dynamic_index_in_dim(piece, which[slot_index], 0, keepdims=False)
        rows_grad = add_upstream_b[slot_index]
        total = jnp.zeros((channels, rows_grad.shape[1]), jnp.float32)
        for plane_index in range(3):
            block = chosen[:, plane_index * 9 * channels : (plane_index + 1) * 9 * channels]
            products = lax.dot_general(
                block, rows_grad, (((0,), (0,)), ((), ())), preferred_element_type=jnp.float32
            )
            for tap_inner in range(9):
                offset = offsets[plane_index * 9 + tap_inner]
                part_rows = products[tap_inner * channels : (tap_inner + 1) * channels]
                total = total + shift_cells(part_rows, -offset[0], -offset[1], -offset[2])
        updates.append(total)
    grad_act = jnp.stack(updates, axis=0)
    grad_start = back_fn(grad_act)[0]
    grad_input = (upstream + grad_start).astype(jnp.bfloat16)
    return (grad_weight, grad_input)


def solution(mesh):
    placed = (
        P(("dp", "fsdp"), None, None),
        P(("dp", "fsdp"), None, None),
        P(("dp", "fsdp")),
        P(("dp", "fsdp")),
        P(),
        P(),
        P(),
        P(None, "fsdp", None),
        P("dp", None),
        P("dp", None),
    )
    return jax.shard_map(
        local,
        mesh=mesh,
        in_specs=placed,
        out_specs=(P(None, "fsdp", None), P(("dp", "fsdp"), None, None)),
        check_vma=False,
    )
```

```python
import functools

import jax
import jax.numpy as jnp
import numpy as np
from jax import lax
from jax.experimental import pallas as pl
from jax.experimental.pallas import tpu as pltpu
from jax.sharding import PartitionSpec as P

GROUPS = 32
SIDE = 16
DEPTH = 4
EPSILON = 1e-05
MESH = pl.DeviceIdType.MESH
RING = 8
C = 96
CELLS = 1024
PLANE = SIDE * SIDE
SPAN = 864
WIDE = 896
TILES = WIDE // 128
ROWS = 36
PACK = (32, WIDE + 128)
BLOCK = 48
OUT_TILES = 64
SHIFTS = [(dy, dz) for dy in (-1, 0, 1) for dz in (-1, 0, 1)]
HOPS = {(0, 0): 4, (0, 1): 3, (1, 0): 3, (1, 1): 4}
F32 = jnp.float32
BF16 = jnp.bfloat16


def bases(first):
    out = {}
    for key, hops in HOPS.items():
        out[key] = first
        first += hops
    return out


def constants():
    main = np.zeros((576, 512), np.float32)
    last = np.zeros((576, 256), np.float32)
    spread = np.zeros((16 * 40, 576), np.float32)
    for s in range(16):
        for q in range(ROWS):
            j, dx, r = q // 18, q % 18 // 6, q % 6
            row = j * 288 + dx * C + 6 * s + r
            if q < 32:
                main[row, 32 * s + q] = 1
            else:
                last[row, 16 * s + q - 32] = 1
                spread[40 * s + q + 4, row] = 1
            spread[40 * s + q, row] = 1
    group = np.kron(np.eye(GROUPS, dtype=np.float32), np.ones((3, 3), np.float32))
    return main, last, spread, group


def rcopy(src, dst, sems, at, device_id):
    return pltpu.make_async_remote_copy(
        src_ref=src,
        dst_ref=dst,
        send_sem=sems[0].at[at],
        recv_sem=sems[1].at[at],
        device_id=device_id,
        device_id_type=MESH,
    )


def column_of(row, eye):
    return jnp.sum(eye * row, axis=1, keepdims=True)


def inside(lane, dy, dz):
    row = lane // SIDE % SIDE
    col = lane % SIDE
    ok = None
    for at, step in ((row, dy), (col, dz)):
        if step != 0:
            one = (at + step >= 0) & (at + step < SIDE)
            ok = one if ok is None else ok & one
    return ok


def pack(rows40):
    half = lax.broadcasted_iota(jnp.int32, (8, 128), 0) < 4
    tail = [rows40[32:40, t * 128 : (t + 1) * 128] for t in range(TILES)] + [
        jnp.zeros((8, 128), F32)
    ]
    last = [jnp.where(half, tail[t], tail[t + 1]) for t in range(0, 8, 2)]
    packed = jnp.concatenate([rows40[:32], jnp.concatenate(last, axis=0)], axis=1)
    return packed.astype(BF16)


def unpack_last(last):
    last = last.astype(F32)
    keep = lax.broadcasted_iota(jnp.int32, (16, 128), 0) < 4
    pieces = []
    for t in range(TILES):
        rolled = last if t == 0 else pltpu.roll(last, 32 - 4 * t, 0)
        pieces.append(jnp.where(keep, rolled[:16], 0.0))
    return jnp.concatenate(pieces, axis=1).astype(BF16)


def kernel(
    chips,
    lat_ref, tgt_ref, reward_ref, step_ref, time_ref, gain_ref, bias_ref, weight_ref, pair_ref,
    count_ref, main_ref, last_ref, spread_ref, group_ref,
    gw_ref, gi_ref,
    got, normed, slope, rstd, cols, both, ups, ucat, fold, part, held, stage, total, swap_out,
    swap_in, table, core_in, half, chunk_in, full,
    ag_s, ag_r, rs_s, rs_r, dp_s, dp_r,
):
    f = lax.axis_index("fsdp")
    z = f // 2
    x = f % 2
    nbr = z * 2 + 1 - x
    up = lax.rem(z + 1, RING) * 2 + x
    down = lax.rem(z + RING - 1, RING) * 2 + x
    d = lax.axis_index("dp")
    core = d % 2
    chip = d // 2
    twin = chip * 2 + 1 - core
    peers = [lax.rem(chip + i, chips) for i in range(1, chips)]
    barrier = pltpu.get_barrier_semaphore()
    for other in (nbr, up, down):
        pl.semaphore_signal(barrier, inc=1, device_id={"fsdp": other}, device_id_type=MESH)
    pl.semaphore_signal(barrier, inc=1, device_id={"dp": twin}, device_id_type=MESH)
    for peer in peers:
        pl.semaphore_signal(
            barrier, inc=1, device_id={"dp": peer * 2 + core}, device_id_type=MESH
        )

    rows = []
    for j in range(2):
        mine = weight_ref[pair_ref[0, j]].astype(F32)
        for dx in range(3):
            rows.append(mine[:, dx * SPAN : (dx + 1) * SPAN])
    stacked = jnp.concatenate(rows, axis=0)
    stacked = jnp.concatenate([stacked, stacked[32:36]], axis=0)
    stacked = jnp.concatenate([stacked, jnp.zeros((40, WIDE - SPAN), F32)], axis=1)
    got[f] = pack(stacked)
    pl.semaphore_wait(barrier, 4 + len(peers))

    ag = (ag_s, ag_r)
    ag_base = bases(1)
    ag_copies = {key: [] for key in HOPS}

    def ag_send(key, h):
        col, direction = key
        zz = lax.rem(z + RING - h, RING) if direction == 0 else lax.rem(z + h, RING)
        item = zz * 2 + (x if col == 0 else 1 - x)
        copy = rcopy(
            got.at[item], got.at[item], ag, ag_base[key] + h,
            {"fsdp": up if direction == 0 else down},
        )
        copy.start()
        ag_copies[key].append(copy)

    def ag_hop(h):
        for key, hops in HOPS.items():
            if h <= hops:
                ag_copies[key][h - 1].wait_recv()
            if h < hops:
                ag_send(key, h)

    swap = rcopy(got.at[f], got.at[f], ag, 0, {"fsdp": nbr})
    swap.start()
    ag_send((0, 0), 0)
    ag_send((0, 1), 0)

    eye = (
        lax.broadcasted_iota(jnp.int32, (C, C), 0) == lax.broadcasted_iota(jnp.int32, (C, C), 1)
    ).astype(F32)
    gain = column_of(gain_ref[...], eye)
    bias = column_of(bias_ref[...], eye)
    lane = lax.broadcasted_iota(jnp.int32, (C, CELLS), 1)

    def group_mean(field):
        sums = jnp.broadcast_to(jnp.sum(field, axis=1, keepdims=True), (C, 128))
        spread = jnp.dot(
            group_ref[...], sums, precision=lax.Precision.HIGHEST, preferred_element_type=F32
        )
        return spread[:, :1] * (1.0 / (3 * CELLS))

    def norm(i):
        start = lat_ref[i].astype(F32) + column_of(time_ref[pl.ds(step_ref[i], 1), :], eye)
        centred = start - group_mean(start)
        scale = lax.rsqrt(group_mean(centred * centred) + EPSILON)
        value = centred * scale
        pre = value * gain + bias
        sig = 1.0 / (1.0 + jnp.exp(-pre))
        normed[i] = value
        slope[i] = sig * (1.0 + pre * (1.0 - sig)) * gain
        rstd[i] = jnp.broadcast_to(scale, (C, 128))
        fold[...] = (pre * sig).astype(BF16).astype(F32)

    def unfold(i):
        act = fold[...]
        for at, (dy, dz) in enumerate(SHIFTS):
            move = 16 * dy + dz
            value = act
            if move != 0:
                value = jnp.where(
                    inside(lane, dy, dz), pltpu.roll(act, (-move) % CELLS, 1), 0.0
                )
            cols[i, at * C : (at + 1) * C, :] = value.astype(BF16)
        cols[i, SPAN:WIDE, :] = jnp.zeros((WIDE - SPAN, CELLS), BF16)

    norm(0)
    swap.wait_recv()
    ag_send((1, 0), 0)
    ag_send((1, 1), 0)
    ag_hop(1)
    unfold(0)
    ag_hop(2)
    norm(1)
    ag_hop(3)
    unfold(1)
    ag_hop(4)
    swap.wait_send()
    for key in HOPS:
        for copy in ag_copies[key]:
            copy.wait_send()

    main = got[:, :, :WIDE].reshape(512, WIDE)
    tails = jnp.concatenate([unpack_last(got[s, :, WIDE:]) for s in range(16)], axis=0)
    kernels = jnp.dot(main_ref[...], main, preferred_element_type=F32) + jnp.dot(
        last_ref[...], tails, preferred_element_type=F32
    )
    both[...] = kernels.astype(BF16).reshape(2, 288, WIDE)

    first, second = count_ref[0, 0], count_ref[0, 1]
    which = []
    grads = []
    zero = jnp.zeros((C, PLANE), F32)
    for i in range(2):
        place = f * 2 + i
        in_first = place < first
        in_second = (place >= first) & (place < first + second)
        which.append(in_second.astype(jnp.int32))
        live = jnp.where(in_first | in_second, reward_ref[i], 0.0)
        taps = jnp.dot(both[which[i]], cols[i], preferred_element_type=F32)
        mixed = (
            jnp.concatenate([zero, taps[:C, :-PLANE]], axis=1)
            + taps[C : 2 * C]
            + jnp.concatenate([taps[2 * C :, PLANE:], zero], axis=1)
        )
        upstream = live * (lat_ref[i].astype(F32) + mixed - tgt_ref[i].astype(F32))
        ups[i] = upstream
        rounded = upstream.astype(BF16)
        none = jnp.zeros((C, PLANE), BF16)
        ucat[i, :C] = jnp.concatenate([rounded[:, PLANE:], none], axis=1)
        ucat[i, C : 2 * C] = rounded
        ucat[i, 2 * C :] = jnp.concatenate([none, rounded[:, :-PLANE]], axis=1)
        grad = lax.dot_general(
            ucat[i], cols[i], (((1,), (1,)), ((), ())), preferred_element_type=F32
        )
        grads.append(
            (
                grad * (jnp.where(in_first, 1.0, 0.0) / CELLS),
                grad * (jnp.where(in_second, 1.0, 0.0) / CELLS),
            )
        )
    sums = jnp.concatenate(
        [(grads[0][j] + grads[1][j]).astype(BF16) for j in range(2)], axis=0
    )
    for block in range(4):
        spread = jnp.dot(
            spread_ref[block * 160 : (block + 1) * 160, :], sums, preferred_element_type=F32
        )
        for s in range(4):
            part[block * 4 + s] = pack(spread[s * 40 : (s + 1) * 40])

    rs = (rs_s, rs_r)
    rs_base = bases(0)
    rs_copies = {key: [] for key in HOPS}

    def rs_hop(h):
        for key, hops in HOPS.items():
            if h >= hops:
                continue
            col, direction = key
            away = hops - h
            zz = lax.rem(z + away, RING) if direction == 0 else lax.rem(z + RING - away, RING)
            at = rs_base[key] + h
            if h == 0:
                src = part.at[zz * 2 + col]
            else:
                rs_copies[key][h - 1].wait_recv()
                stage[at] = (
                    held[at - 1].astype(F32) + part[zz * 2 + col].astype(F32)
                ).astype(BF16)
                src = stage.at[at]
            copy = rcopy(src, held.at[at], rs, at, {"fsdp": up if direction == 0 else down})
            copy.start()
            rs_copies[key].append(copy)

    def back(i):
        products = lax.dot_general(
            both[which[i]], ucat[i], (((0,), (0,)), ((), ())), preferred_element_type=F32
        )
        acc = products[4 * C : 5 * C]
        for at, (dy, dz) in enumerate(SHIFTS):
            move = 16 * dy + dz
            if move != 0:
                piece = products[at * C : (at + 1) * C]
                acc = acc + jnp.where(
                    inside(lane, -dy, -dz), pltpu.roll(piece, move % CELLS, 1), 0.0
                )
        fold[...] = acc

    def finish(i):
        value = normed[i]
        flow = fold[...] * slope[i]
        start = rstd[i][:, :1] * (flow - group_mean(flow) - value * group_mean(flow * value))
        gi_ref[i] = (ups[i] + start).astype(BF16)

    rs_hop(0)
    back(0)
    rs_hop(1)
    finish(0)
    rs_hop(2)
    back(1)
    rs_hop(3)
    finish(1)
    for col in (0, 1):
        rs_copies[(col, 0)][-1].wait_recv()
        rs_copies[(col, 1)][-1].wait_recv()
        value = (
            part[z * 2 + col].astype(F32)
            + held[rs_base[(col, 0)] + HOPS[(col, 0)] - 1].astype(F32)
            + held[rs_base[(col, 1)] + HOPS[(col, 1)] - 1].astype(F32)
        )
        total[col] = value
        swap_out[col] = value.astype(BF16)
    cross = rcopy(swap_out.at[1 - x], swap_in, rs, 14, {"fsdp": nbr})
    cross.start()
    cross.wait_recv()
    lane_sum = (total[x] + swap_in[...].astype(F32)).astype(BF16)
    lane_sum = jnp.concatenate([lane_sum[:, :WIDE], unpack_last(lane_sum[:, WIDE:])], axis=0)
    row = lax.broadcasted_iota(jnp.int32, (144, BLOCK), 0)
    col = lax.broadcasted_iota(jnp.int32, (144, BLOCK), 1)
    ahead = jnp.where(col < 18, pair_ref[0, 0] * 18, pair_ref[0, 1] * 18 - 18)
    choose = ((row - col == ahead) & (col < ROWS)).astype(F32).astype(BF16)
    wide = jnp.dot(choose, lane_sum, preferred_element_type=F32).astype(BF16)
    for r in range(9):
        for t in range(TILES):
            table[r * TILES + t] = wide[r * 16 : (r + 1) * 16, t * 128 : (t + 1) * 128]
    table[OUT_TILES - 1] = jnp.zeros((16, 128), BF16)

    dp = (dp_s, dp_r)
    own_half = OUT_TILES // 2
    share = own_half // chips
    first_tile = core * own_half
    pair = rcopy(
        table.at[pl.ds(own_half - first_tile, own_half)], core_in, dp, 30, {"dp": twin}
    )
    pair.start()
    pair.wait_recv()
    half[...] = (
        table[pl.ds(first_tile, own_half)].astype(F32) + core_in[...].astype(F32)
    ).astype(BF16)
    scatters = []
    for i, peer in enumerate(peers):
        copy = rcopy(
            half.at[pl.ds(peer * share, share)], chunk_in.at[i], dp, i,
            {"dp": peer * 2 + core},
        )
        copy.start()
        scatters.append(copy)
    acc = half[pl.ds(chip * share, share)].astype(F32)
    for i, copy in enumerate(scatters):
        copy.wait_recv()
        acc = acc + chunk_in[i].astype(F32)
    own = pl.ds(first_tile + chip * share, share)
    full[own] = acc.astype(BF16)
    gathers = []
    for i, peer in enumerate(peers):
        copy = rcopy(full.at[own], full.at[own], dp, 15 + i, {"dp": peer * 2 + core})
        copy.start()
        gathers.append(copy)
    for copy in gathers:
        copy.wait_recv()
    mine = pl.ds(first_tile, own_half)
    last = rcopy(full.at[mine], full.at[mine], dp, 31, {"dp": twin})
    last.start()
    last.wait_recv()
    lines = jnp.concatenate(
        [
            jnp.concatenate([full[r * TILES + t].astype(F32) for t in range(TILES)], axis=1)
            for r in range(9)
        ],
        axis=0,
    )
    for e in range(8):
        for dx in range(3):
            at = e * 18 + dx * 6
            gw_ref[e, :, dx * SPAN : (dx + 1) * SPAN] = lines[at : at + 6, :SPAN]
    for key in HOPS:
        for copy in rs_copies[key]:
            copy.wait_send()
    for copy in [cross, pair, last] + scatters + gathers:
        copy.wait_send()


def local(
    chips,
    latents,
    targets,
    rewards,
    time_steps,
    time_table,
    norm_gain,
    norm_bias,
    expert_weights,
    lane_experts,
    lane_counts,
):
    main, last, spread, group = constants()
    vmem = pl.BlockSpec(memory_space=pltpu.VMEM)
    smem = pl.BlockSpec(memory_space=pltpu.SMEM)
    sems = pltpu.SemaphoreType.DMA
    return pl.pallas_call(
        functools.partial(kernel, chips),
        out_shape=(
            jax.ShapeDtypeStruct((8, 6, 3 * SPAN), F32),
            jax.ShapeDtypeStruct((2, C, CELLS), BF16),
        ),
        in_specs=[vmem, vmem, smem, smem, vmem, vmem, vmem, vmem, smem, smem] + [vmem] * 4,
        out_specs=(vmem, vmem),
        scratch_shapes=[
            pltpu.VMEM((16,) + PACK, BF16),
            pltpu.VMEM((2, C, CELLS), F32),
            pltpu.VMEM((2, C, CELLS), F32),
            pltpu.VMEM((2, C, 128), F32),
            pltpu.VMEM((2, WIDE, CELLS), BF16),
            pltpu.VMEM((2, 288, WIDE), BF16),
            pltpu.VMEM((2, C, CELLS), F32),
            pltpu.VMEM((2, 288, CELLS), BF16),
            pltpu.VMEM((C, CELLS), F32),
            pltpu.VMEM((16,) + PACK, BF16),
            pltpu.VMEM((14,) + PACK, BF16),
            pltpu.VMEM((14,) + PACK, BF16),
            pltpu.VMEM((2,) + PACK, F32),
            pltpu.VMEM((2,) + PACK, BF16),
            pltpu.VMEM(PACK, BF16),
            pltpu.VMEM((OUT_TILES, 16, 128), BF16),
            pltpu.VMEM((OUT_TILES // 2, 16, 128), BF16),
            pltpu.VMEM((OUT_TILES // 2, 16, 128), BF16),
            pltpu.VMEM((15, OUT_TILES // 2 // chips, 16, 128), BF16),
            pltpu.VMEM((OUT_TILES, 16, 128), BF16),
            sems((15,)),
            sems((15,)),
            sems((15,)),
            sems((15,)),
            sems((32,)),
            sems((32,)),
        ],
        compiler_params=pltpu.CompilerParams(
            collective_id=0, has_side_effects=True, vmem_limit_bytes=50 * 2**20
        ),
    )(
        latents, targets, rewards, time_steps, time_table, norm_gain[None, :],
        norm_bias[None, :], expert_weights, lane_experts, lane_counts,
        jnp.asarray(main, BF16), jnp.asarray(last, BF16), jnp.asarray(spread, BF16),
        jnp.asarray(group, F32),
    )


def solution(mesh):
    placed = (
        P(("dp", "fsdp"), None, None),
        P(("dp", "fsdp"), None, None),
        P(("dp", "fsdp")),
        P(("dp", "fsdp")),
        P(),
        P(),
        P(),
        P(None, "fsdp", None),
        P("dp", None),
        P("dp", None),
    )
    return jax.shard_map(
        functools.partial(local, mesh.shape["dp"] // 2),
        mesh=mesh,
        in_specs=placed,
        out_specs=(P(None, "fsdp", None), P(("dp", "fsdp"), None, None)),
        check_vma=False,
    )
```

```python
import functools

import jax
import jax.numpy as jnp
import numpy as np
from jax import lax
from jax.experimental import pallas as pl
from jax.experimental.pallas import tpu as pltpu
from jax.sharding import PartitionSpec as P

GROUPS = 32
SIDE = 16
DEPTH = 4
EPSILON = 1e-05
MESH = pl.DeviceIdType.MESH
RING = 8
C = 96
CELLS = 1024
PLANE = SIDE * SIDE
SPAN = 864
WIDE = 896
TILES = WIDE // 128
ROWS = 36
PACK = (32, WIDE + 128)
BLOCK = 48
OUT_TILES = 64
SHIFTS = [(dy, dz) for dy in (-1, 0, 1) for dz in (-1, 0, 1)]
AWAY = (4, 3, 5, 2, 6, 1, 7)
NEAR = (1, 7, 2, 6, 3, 5, 4)
F32 = jnp.float32
BF16 = jnp.bfloat16


def constants():
    main = np.zeros((576, 512), np.float32)
    last = np.zeros((576, 256), np.float32)
    spread = np.zeros((16 * 40, 576), np.float32)
    for s in range(16):
        for q in range(ROWS):
            dx, j, r = q // 12, q % 12 // 6, q % 6
            row = j * 288 + dx * C + 6 * s + r
            if q < 32:
                main[row, 32 * s + q] = 1
            else:
                last[row, 16 * s + q - 32] = 1
                spread[40 * s + q + 4, row] = 1
            spread[40 * s + q, row] = 1
    group = np.kron(np.eye(GROUPS, dtype=np.float32), np.ones((3, 3), np.float32))
    return main, last, spread, group


def rcopy(src, dst, sems, at, device_id):
    return pltpu.make_async_remote_copy(
        src_ref=src,
        dst_ref=dst,
        send_sem=sems[0].at[at],
        recv_sem=sems[1].at[at],
        device_id=device_id,
        device_id_type=MESH,
    )


def column_of(row, eye):
    return jnp.sum(eye * row, axis=1, keepdims=True)


def inside(lane, dy, dz):
    row = lane // SIDE % SIDE
    col = lane % SIDE
    ok = None
    for at, step in ((row, dy), (col, dz)):
        if step != 0:
            one = (at + step >= 0) & (at + step < SIDE)
            ok = one if ok is None else ok & one
    return ok


def pack(rows40):
    half = lax.broadcasted_iota(jnp.int32, (8, 128), 0) < 4
    tail = [rows40[32:40, t * 128 : (t + 1) * 128] for t in range(TILES)] + [
        jnp.zeros((8, 128), F32)
    ]
    last = [jnp.where(half, tail[t], tail[t + 1]) for t in range(0, 8, 2)]
    packed = jnp.concatenate([rows40[:32], jnp.concatenate(last, axis=0)], axis=1)
    return packed.astype(BF16)


def unpack_last(last):
    last = last.astype(F32)
    keep = lax.broadcasted_iota(jnp.int32, (16, 128), 0) < 4
    pieces = []
    for t in range(TILES):
        rolled = last if t == 0 else pltpu.roll(last, 32 - 4 * t, 0)
        pieces.append(jnp.where(keep, rolled[:16], 0.0))
    return jnp.concatenate(pieces, axis=1).astype(BF16)


def kernel(
    chips,
    lat_hbm, tgt_hbm, reward_ref, step_ref, time_hbm, gain_ref, bias_ref, weight_hbm, pair_ref,
    count_ref, main_hbm, last_hbm, spread_hbm, group_hbm,
    gw_ref, gi_hbm,
    gi_ref, weight_ref, lat_ref, tgt_ref, time_ref, main_ref, last_ref, spread_ref, group_ref,
    got, normed, slope, rstd, cols, both, ups, ucat, fold, part, x_in, held, stage, table,
    core_in, half, chunk_in, full,
    ag_s, ag_r, rs_s, rs_r, dp_s, dp_r, in_s,
):
    f = lax.axis_index("fsdp")
    z = f // 2
    x = f % 2
    nbr = z * 2 + 1 - x
    d = lax.axis_index("dp")
    core = d % 2
    chip = d // 2
    twin = chip * 2 + 1 - core
    peers = [lax.rem(chip + i, chips) for i in range(1, chips)]
    ring = {k: lax.rem(z + k, RING) for k in range(RING)}
    barrier = pltpu.get_barrier_semaphore()
    for other in [nbr] + [ring[k] * 2 + x for k in NEAR]:
        pl.semaphore_signal(barrier, inc=1, device_id={"fsdp": other}, device_id_type=MESH)
    pl.semaphore_signal(barrier, inc=1, device_id={"dp": twin}, device_id_type=MESH)
    for peer in peers:
        pl.semaphore_signal(
            barrier, inc=1, device_id={"dp": peer * 2 + core}, device_id_type=MESH
        )
    inputs = {}
    for at, (name, src, dst) in enumerate((
        ("weight", weight_hbm, weight_ref), ("lat", lat_hbm, lat_ref), ("time", time_hbm, time_ref), ("group", group_hbm, group_ref),
        ("main", main_hbm, main_ref), ("last", last_hbm, last_ref), ("tgt", tgt_hbm, tgt_ref),
        ("spread", spread_hbm, spread_ref),
    )):
        inputs[name] = pltpu.make_async_copy(src, dst, in_s.at[at])
        inputs[name].start()

    row = lax.broadcasted_iota(jnp.int32, (16, 48), 0)
    col = lax.broadcasted_iota(jnp.int32, (16, 48), 1)
    expert = jnp.where(row < 6, pair_ref[0, 0], pair_ref[0, 1] - 48)
    pick = ((col - 8 * row == expert) & (row < 12)).astype(F32).astype(BF16)
    inputs["weight"].wait()
    mine = jnp.dot(pick, weight_ref[...], preferred_element_type=F32)[:12]
    rows = [mine[:, dx * SPAN : (dx + 1) * SPAN] for dx in range(3)]
    rows.append(rows[2][8:12])
    stacked = jnp.concatenate(rows, axis=0)
    stacked = jnp.concatenate([stacked, jnp.zeros((40, WIDE - SPAN), F32)], axis=1)
    got[f] = pack(stacked)
    pl.semaphore_wait(barrier, RING + 1 + len(peers))

    ag = (ag_s, ag_r)
    swap = rcopy(got.at[f], got.at[f], ag, 7, {"fsdp": nbr})
    direct = []
    for i, k in enumerate(NEAR):
        copy = rcopy(got.at[f], got.at[f], ag, i, {"fsdp": ring[k] * 2 + x})
        copy.start()
        direct.append(copy)
        if i == 1:
            swap.start()
    passed = []

    def hand_on(count):
        for i in range(len(passed), len(passed) + count):
            direct[i].wait_recv()
            item = ring[RING - NEAR[i]] * 2 + x
            copy = rcopy(got.at[item], got.at[item], ag, 8 + i, {"fsdp": nbr})
            copy.start()
            passed.append(copy)

    eye = (
        lax.broadcasted_iota(jnp.int32, (C, C), 0) == lax.broadcasted_iota(jnp.int32, (C, C), 1)
    ).astype(F32)
    gain = column_of(gain_ref[...], eye)
    bias = column_of(bias_ref[...], eye)
    lane = lax.broadcasted_iota(jnp.int32, (C, CELLS), 1)
    moment = lax.broadcasted_iota(jnp.int32, time_ref.shape, 1)

    def group_mean(field):
        sums = jnp.broadcast_to(jnp.sum(field, axis=1, keepdims=True), (C, 128))
        spread = jnp.dot(
            group_ref[...], sums, precision=lax.Precision.HIGHEST, preferred_element_type=F32
        )
        return spread[:, :1] * (1.0 / (3 * CELLS))

    def norm(i):
        start = lat_ref[i].astype(F32) + jnp.sum(
            jnp.where(moment == step_ref[i], time_ref[...], 0.0), axis=1, keepdims=True
        )
        centred = start - group_mean(start)
        scale = lax.rsqrt(group_mean(centred * centred) + EPSILON)
        value = centred * scale
        pre = value * gain + bias
        sig = 1.0 / (1.0 + jnp.exp(-pre))
        normed[i] = value
        slope[i] = sig * (1.0 + pre * (1.0 - sig)) * gain
        rstd[i] = jnp.broadcast_to(scale, (C, 128))
        fold[...] = (pre * sig).astype(BF16).astype(F32)

    def unfold(i):
        act = fold[...]
        for at, (dy, dz) in enumerate(SHIFTS):
            move = 16 * dy + dz
            value = act
            if move != 0:
                value = jnp.where(
                    inside(lane, dy, dz), pltpu.roll(act, (-move) % CELLS, 1), 0.0
                )
            cols[i, at * C : (at + 1) * C, :] = value.astype(BF16)
        cols[i, SPAN:WIDE, :] = jnp.zeros((WIDE - SPAN, CELLS), BF16)

    for name in ("lat", "time", "group"):
        inputs[name].wait()
    norm(0)
    unfold(0)
    hand_on(4)
    norm(1)
    hand_on(2)
    unfold(1)
    hand_on(1)
    for name in ("main", "last", "tgt", "spread"):
        inputs[name].wait()
    for copy in [swap] + passed:
        copy.wait_recv()
    for copy in [swap] + direct + passed:
        copy.wait_send()

    main = got[:, :, :WIDE].reshape(512, WIDE)
    tails = jnp.concatenate([unpack_last(got[s, :, WIDE:]) for s in range(16)], axis=0)
    kernels = jnp.dot(main_ref[...], main, preferred_element_type=F32) + jnp.dot(
        last_ref[...], tails, preferred_element_type=F32
    )
    both[...] = kernels.astype(BF16).reshape(2, 288, WIDE)

    first, second = count_ref[0, 0], count_ref[0, 1]
    which = []
    grads = []
    zero = jnp.zeros((C, PLANE), F32)
    for i in range(2):
        place = f * 2 + i
        in_first = place < first
        in_second = (place >= first) & (place < first + second)
        which.append(in_second.astype(jnp.int32))
        live = jnp.where(in_first | in_second, reward_ref[i], 0.0)
        taps = jnp.dot(both[which[i]], cols[i], preferred_element_type=F32)
        mixed = (
            jnp.concatenate([zero, taps[:C, :-PLANE]], axis=1)
            + taps[C : 2 * C]
            + jnp.concatenate([taps[2 * C :, PLANE:], zero], axis=1)
        )
        upstream = live * (lat_ref[i].astype(F32) + mixed - tgt_ref[i].astype(F32))
        ups[i] = upstream
        rounded = upstream.astype(BF16)
        none = jnp.zeros((C, PLANE), BF16)
        ucat[i, :C] = jnp.concatenate([rounded[:, PLANE:], none], axis=1)
        ucat[i, C : 2 * C] = rounded
        ucat[i, 2 * C :] = jnp.concatenate([none, rounded[:, :-PLANE]], axis=1)
        grad = lax.dot_general(
            ucat[i], cols[i], (((1,), (1,)), ((), ())), preferred_element_type=F32
        )
        grads.append(
            (
                grad * (jnp.where(in_first, 1.0, 0.0) / CELLS),
                grad * (jnp.where(in_second, 1.0, 0.0) / CELLS),
            )
        )
    sums = jnp.concatenate(
        [(grads[0][j] + grads[1][j]).astype(BF16) for j in range(2)], axis=0
    )
    for block in range(4):
        spread = jnp.dot(
            spread_ref[block * 160 : (block + 1) * 160, :], sums, preferred_element_type=F32
        )
        for s in range(4):
            part[block * 4 + s] = pack(spread[s * 40 : (s + 1) * 40])

    rs = (rs_s, rs_r)
    order = AWAY + (0,)
    crosses = []
    for i, k in enumerate(order):
        copy = rcopy(part.at[ring[k] * 2 + 1 - x], x_in.at[i], rs, i, {"fsdp": nbr})
        copy.start()
        crosses.append(copy)
    sends = []

    def send_on(count):
        for i in range(len(sends), len(sends) + count):
            crosses[i].wait_recv()
            stage[i] = (part[ring[AWAY[i]] * 2 + x].astype(F32) + x_in[i].astype(F32)).astype(
                BF16
            )
            copy = rcopy(
                stage.at[i], held.at[i], rs, 8 + i, {"fsdp": ring[AWAY[i]] * 2 + x}
            )
            copy.start()
            sends.append(copy)

    def back(i):
        products = lax.dot_general(
            both[which[i]], ucat[i], (((0,), (0,)), ((), ())), preferred_element_type=F32
        )
        acc = products[4 * C : 5 * C]
        for at, (dy, dz) in enumerate(SHIFTS):
            move = 16 * dy + dz
            if move != 0:
                piece = products[at * C : (at + 1) * C]
                acc = acc + jnp.where(
                    inside(lane, -dy, -dz), pltpu.roll(piece, move % CELLS, 1), 0.0
                )
        fold[...] = acc

    results = []

    def finish(i):
        value = normed[i]
        flow = fold[...] * slope[i]
        start = rstd[i][:, :1] * (flow - group_mean(flow) - value * group_mean(flow * value))
        gi_ref[i] = (ups[i] + start).astype(BF16)
        result = pltpu.make_async_copy(gi_ref.at[i], gi_hbm.at[i], in_s.at[8 + i])
        result.start()
        results.append(result)

    back(0)
    send_on(4)
    finish(0)
    send_on(3)
    back(1)
    finish(1)
    crosses[7].wait_recv()
    lane_sum = part[f].astype(F32) + x_in[7].astype(F32)
    for i, copy in enumerate(sends):
        copy.wait_recv()
        lane_sum = lane_sum + held[i].astype(F32)
    lane_sum = lane_sum.astype(BF16)
    lane_sum = jnp.concatenate([lane_sum[:, :WIDE], unpack_last(lane_sum[:, WIDE:])], axis=0)
    row = lax.broadcasted_iota(jnp.int32, (144, BLOCK), 0)
    col = lax.broadcasted_iota(jnp.int32, (144, BLOCK), 1)
    expert = jnp.where(col % 12 < 6, pair_ref[0, 0], pair_ref[0, 1])
    choose = (
        (row // 48 == col // 12) & (row % 48 // 8 == col % 6) & (row % 8 == expert)
    ).astype(F32).astype(BF16)
    wide = jnp.dot(choose, lane_sum, preferred_element_type=F32).astype(BF16)
    for r in range(9):
        for t in range(TILES):
            table[r * TILES + t] = wide[r * 16 : (r + 1) * 16, t * 128 : (t + 1) * 128]
    table[OUT_TILES - 1] = jnp.zeros((16, 128), BF16)

    dp = (dp_s, dp_r)
    own_half = OUT_TILES // 2
    share = own_half // chips
    first_tile = core * own_half
    pair = rcopy(
        table.at[pl.ds(own_half - first_tile, own_half)], core_in, dp, 30, {"dp": twin}
    )
    pair.start()
    pair.wait_recv()
    half[...] = (
        table[pl.ds(first_tile, own_half)].astype(F32) + core_in[...].astype(F32)
    ).astype(BF16)
    scatters = []
    for i, peer in enumerate(peers):
        copy = rcopy(
            half.at[pl.ds(peer * share, share)], chunk_in.at[i], dp, i,
            {"dp": peer * 2 + core},
        )
        copy.start()
        scatters.append(copy)
    acc = half[pl.ds(chip * share, share)].astype(F32)
    for i, copy in enumerate(scatters):
        copy.wait_recv()
        acc = acc + chunk_in[i].astype(F32)
    own = pl.ds(first_tile + chip * share, share)
    full[own] = acc.astype(BF16)
    gathers = []
    for i, peer in enumerate(peers):
        copy = rcopy(full.at[own], full.at[own], dp, 15 + i, {"dp": peer * 2 + core})
        copy.start()
        gathers.append(copy)
    for copy in gathers:
        copy.wait_recv()
    mine = pl.ds(first_tile, own_half)
    last = rcopy(full.at[mine], full.at[mine], dp, 31, {"dp": twin})
    last.start()
    last.wait_recv()
    for dx in range(3):
        for r in range(6):
            at = dx * 6 + r
            line = jnp.concatenate(
                [full[at // 2 * TILES + t].astype(F32)[at % 2 * 8 :][:8] for t in range(TILES)],
                axis=1,
            )
            gw_ref[r, :, dx * SPAN : (dx + 1) * SPAN] = line[:, :SPAN]
    for copy in results:
        copy.wait()
    for copy in crosses + sends + [pair, last] + scatters + gathers:
        copy.wait_send()


def local(
    chips,
    latents,
    targets,
    rewards,
    time_steps,
    time_table,
    norm_gain,
    norm_bias,
    expert_weights,
    lane_experts,
    lane_counts,
):
    main, last, spread, group = constants()
    vmem = pl.BlockSpec(memory_space=pltpu.VMEM)
    smem = pl.BlockSpec(memory_space=pltpu.SMEM)
    sems = pltpu.SemaphoreType.DMA
    hbm = pl.BlockSpec(memory_space=pltpu.MemorySpace.HBM)
    grad_weight, grad_input = pl.pallas_call(
        functools.partial(kernel, chips),
        out_shape=(
            jax.ShapeDtypeStruct((6, 8, 3 * SPAN), F32),
            jax.ShapeDtypeStruct((2, C, CELLS), BF16),
        ),
        in_specs=[hbm, hbm, smem, smem, hbm, vmem, vmem, hbm, smem, smem] + [hbm] * 4,
        out_specs=(vmem, hbm),
        scratch_shapes=[
            pltpu.VMEM((2, C, CELLS), BF16),
            pltpu.VMEM((48, 3 * SPAN), BF16),
            pltpu.VMEM((2, C, CELLS), BF16),
            pltpu.VMEM((2, C, CELLS), BF16),
            pltpu.VMEM(time_table.shape[::-1], F32),
            pltpu.VMEM(main.shape, BF16),
            pltpu.VMEM(last.shape, BF16),
            pltpu.VMEM(spread.shape, BF16),
            pltpu.VMEM(group.shape, F32),
            pltpu.VMEM((16,) + PACK, BF16),
            pltpu.VMEM((2, C, CELLS), F32),
            pltpu.VMEM((2, C, CELLS), F32),
            pltpu.VMEM((2, C, 128), F32),
            pltpu.VMEM((2, WIDE, CELLS), BF16),
            pltpu.VMEM((2, 288, WIDE), BF16),
            pltpu.VMEM((2, C, CELLS), F32),
            pltpu.VMEM((2, 288, CELLS), BF16),
            pltpu.VMEM((C, CELLS), F32),
            pltpu.VMEM((16,) + PACK, BF16),
            pltpu.VMEM((8,) + PACK, BF16),
            pltpu.VMEM((7,) + PACK, BF16),
            pltpu.VMEM((7,) + PACK, BF16),
            pltpu.VMEM((OUT_TILES, 16, 128), BF16),
            pltpu.VMEM((OUT_TILES // 2, 16, 128), BF16),
            pltpu.VMEM((OUT_TILES // 2, 16, 128), BF16),
            pltpu.VMEM((15, OUT_TILES // 2 // chips, 16, 128), BF16),
            pltpu.VMEM((OUT_TILES, 16, 128), BF16),
            sems((15,)),
            sems((15,)),
            sems((15,)),
            sems((15,)),
            sems((32,)),
            sems((32,)),
            sems((10,)),
        ],
        compiler_params=pltpu.CompilerParams(
            collective_id=0, has_side_effects=True, vmem_limit_bytes=60 * 2**20
        ),
    )(
        latents, targets, rewards, time_steps, time_table.T, norm_gain[None, :],
        norm_bias[None, :], expert_weights.swapaxes(0, 1).reshape(48, 3 * SPAN), lane_experts,
        lane_counts,
        jnp.asarray(main, BF16), jnp.asarray(last, BF16), jnp.asarray(spread, BF16),
        jnp.asarray(group, F32),
    )
    return grad_weight.swapaxes(0, 1), grad_input


def solution(mesh):
    placed = (
        P(("dp", "fsdp"), None, None),
        P(("dp", "fsdp"), None, None),
        P(("dp", "fsdp")),
        P(("dp", "fsdp")),
        P(),
        P(),
        P(),
        P(None, "fsdp", None),
        P("dp", None),
        P("dp", None),
    )
    return jax.shard_map(
        functools.partial(local, mesh.shape["dp"] // 2),
        mesh=mesh,
        in_specs=placed,
        out_specs=(P(None, "fsdp", None), P(("dp", "fsdp"), None, None)),
        check_vma=False,
    )
```

```python
import functools

import jax
import jax.numpy as jnp
import numpy as np
from jax import lax
from jax.experimental import pallas as pl
from jax.experimental.pallas import tpu as pltpu
from jax.sharding import PartitionSpec as P

GROUPS = 32
SIDE = 16
DEPTH = 4
EPSILON = 1e-05
MESH = pl.DeviceIdType.MESH
RING = 8
C = 96
CELLS = 1024
PLANE = SIDE * SIDE
SPAN = 864
WIDE = 896
TILES = WIDE // 128
ROWS = 36
PACK = (32, WIDE + 128)
BLOCK = 48
OUT_TILES = 64
SHIFTS = [(dy, dz) for dy in (-1, 0, 1) for dz in (-1, 0, 1)]
F32 = jnp.float32
BF16 = jnp.bfloat16


def constants():
    main = np.zeros((576, 512), np.float32)
    last = np.zeros((576, 256), np.float32)
    spread = np.zeros((16 * 40, 576), np.float32)
    for s in range(16):
        for q in range(ROWS):
            dx, j, r = q // 12, q % 12 // 6, q % 6
            row = j * 288 + dx * C + 6 * s + r
            if q < 32:
                main[row, 32 * s + q] = 1
            else:
                last[row, 16 * s + q - 32] = 1
                spread[40 * s + q + 4, row] = 1
            spread[40 * s + q, row] = 1
    group = np.kron(np.eye(GROUPS, dtype=np.float32), np.ones((3, 3), np.float32))
    return main, last, np.concatenate([spread, spread]), group


def rcopy(src, dst, sems, at, device_id):
    return pltpu.make_async_remote_copy(
        src_ref=src,
        dst_ref=dst,
        send_sem=sems[0].at[at],
        recv_sem=sems[1].at[at],
        device_id=device_id,
        device_id_type=MESH,
    )


def column_of(row, eye):
    return jnp.sum(eye * row, axis=1, keepdims=True)


def inside(lane, dy, dz):
    row = lane // SIDE % SIDE
    col = lane % SIDE
    ok = None
    for at, step in ((row, dy), (col, dz)):
        if step != 0:
            one = (at + step >= 0) & (at + step < SIDE)
            ok = one if ok is None else ok & one
    return ok


def pack(rows40):
    half = lax.broadcasted_iota(jnp.int32, (8, 128), 0) < 4
    tail = [rows40[32:40, t * 128 : (t + 1) * 128] for t in range(TILES)] + [
        jnp.zeros((8, 128), F32)
    ]
    last = [jnp.where(half, tail[t], tail[t + 1]) for t in range(0, 8, 2)]
    packed = jnp.concatenate([rows40[:32], jnp.concatenate(last, axis=0)], axis=1)
    return packed.astype(BF16)


def unpack_last(last):
    last = last.astype(F32)
    keep = lax.broadcasted_iota(jnp.int32, (16, 128), 0) < 4
    pieces = []
    for t in range(TILES):
        rolled = last if t == 0 else pltpu.roll(last, 32 - 4 * t, 0)
        pieces.append(jnp.where(keep, rolled[:16], 0.0))
    return jnp.concatenate(pieces, axis=1).astype(BF16)


def kernel(
    chips,
    lat_hbm, tgt_hbm, reward_ref, step_ref, time_hbm, gain_ref, bias_ref, weight_hbm, pair_ref,
    count_ref, main_hbm, last_hbm, spread_hbm, group_hbm,
    full, gi_hbm,
    gi_ref, weight_ref, lat_ref, tgt_ref, time_ref, main_ref, last_ref, spread_ref, group_ref,
    got, normed, slope, rstd, cols, both, ups, ucat, fold, part, landed, stage,
    choose_out, choose_in, lane_out, lane_in, table, chunk_in,
    ag_s, ag_r, rs_s, rs_r, dp_s, dp_r, in_s,
):
    f = lax.axis_index("fsdp")
    z = f // 2
    x = f % 2
    nbr = z * 2 + 1 - x
    d = lax.axis_index("dp")
    core = d % 2
    chip = d // 2
    twin = chip * 2 + 1 - core
    peers = [lax.rem(chip + i, chips) for i in range(1, chips)]
    ring = {k: lax.rem(z + k, RING) for k in range(RING)}
    barrier = pltpu.get_barrier_semaphore()
    for other in [nbr] + [ring[k] * 2 + x for k in (1, 7, 2, 6)]:
        pl.semaphore_signal(barrier, inc=1, device_id={"fsdp": other}, device_id_type=MESH)
    pl.semaphore_signal(barrier, inc=1, device_id={"dp": twin}, device_id_type=MESH)
    for peer in peers:
        pl.semaphore_signal(
            barrier, inc=1, device_id={"dp": peer * 2 + core}, device_id_type=MESH
        )
    inputs = {}
    for at, (name, src, dst) in enumerate((
        ("weight", weight_hbm, weight_ref), ("lat", lat_hbm, lat_ref),
        ("time", time_hbm, time_ref), ("group", group_hbm, group_ref),
        ("main", main_hbm, main_ref), ("last", last_hbm, last_ref), ("tgt", tgt_hbm, tgt_ref),
        ("spread", spread_hbm, spread_ref),
    )):
        inputs[name] = pltpu.make_async_copy(src, dst, in_s.at[at])
        inputs[name].start()

    row = lax.broadcasted_iota(jnp.int32, (16, 48), 0)
    col = lax.broadcasted_iota(jnp.int32, (16, 48), 1)
    expert = jnp.where(row < 6, pair_ref[0, 0], pair_ref[0, 1] - 48)
    pick = ((col - 8 * row == expert) & (row < 12)).astype(F32).astype(BF16)
    inputs["weight"].wait()
    mine = jnp.dot(pick, weight_ref[...], preferred_element_type=F32)[:12]
    rows = [mine[:, dx * SPAN : (dx + 1) * SPAN] for dx in range(3)]
    rows.append(rows[2][8:12])
    stacked = jnp.concatenate(rows, axis=0)
    stacked = jnp.concatenate([stacked, jnp.zeros((40, WIDE - SPAN), F32)], axis=1)
    got[f] = pack(stacked)
    pl.semaphore_wait(barrier, 6 + len(peers))

    row = lax.broadcasted_iota(jnp.int32, (144, BLOCK), 0)
    col = lax.broadcasted_iota(jnp.int32, (144, BLOCK), 1)
    expert = jnp.where(col % 12 < 6, pair_ref[0, 0], pair_ref[0, 1])
    choose_out[...] = (
        (row // 48 == col // 12) & (row % 48 // 8 == col % 6) & (row % 8 == expert)
    ).astype(F32).astype(BF16)

    ag_copies = {}

    def pass_on(name, item, to):
        at = len(ag_copies)
        copy = rcopy(got.at[item], got.at[item], (ag_s, ag_r), at, {"fsdp": to})
        copy.start()
        ag_copies[name] = copy

    def shard(k):
        return ring[k] * 2 + x

    pass_on("swap", f, nbr)
    for k in (2, 6, 1, 7):
        pass_on(k, f, shard(k))
    told = rcopy(choose_out, choose_in, (dp_s, dp_r), 32, {"dp": twin})
    told.start()

    eye = (
        lax.broadcasted_iota(jnp.int32, (C, C), 0) == lax.broadcasted_iota(jnp.int32, (C, C), 1)
    ).astype(F32)
    gain = column_of(gain_ref[...], eye)
    bias = column_of(bias_ref[...], eye)
    lane = lax.broadcasted_iota(jnp.int32, (C, CELLS), 1)
    moment = lax.broadcasted_iota(jnp.int32, time_ref.shape, 1)

    def group_mean(field):
        sums = jnp.broadcast_to(jnp.sum(field, axis=1, keepdims=True), (C, 128))
        spread = jnp.dot(
            group_ref[...], sums, precision=lax.Precision.HIGHEST, preferred_element_type=F32
        )
        return spread[:, :1] * (1.0 / (3 * CELLS))

    def norm(i):
        start = lat_ref[i].astype(F32) + jnp.sum(
            jnp.where(moment == step_ref[i], time_ref[...], 0.0), axis=1, keepdims=True
        )
        centred = start - group_mean(start)
        scale = lax.rsqrt(group_mean(centred * centred) + EPSILON)
        value = centred * scale
        pre = value * gain + bias
        sig = 1.0 / (1.0 + jnp.exp(-pre))
        normed[i] = value
        slope[i] = sig * (1.0 + pre * (1.0 - sig)) * gain
        rstd[i] = jnp.broadcast_to(scale, (C, 128))
        fold[...] = (pre * sig).astype(BF16).astype(F32)

    def unfold(i):
        act = fold[...]
        for at, (dy, dz) in enumerate(SHIFTS):
            move = 16 * dy + dz
            value = act
            if move != 0:
                value = jnp.where(
                    inside(lane, dy, dz), pltpu.roll(act, (-move) % CELLS, 1), 0.0
                )
            cols[i, at * C : (at + 1) * C, :] = value.astype(BF16)
        cols[i, SPAN:WIDE, :] = jnp.zeros((WIDE - SPAN, CELLS), BF16)

    for name in ("lat", "time", "group"):
        inputs[name].wait()
    norm(0)
    unfold(0)
    ag_copies["swap"].wait_recv()
    pass_on("next", nbr, shard(1))
    pass_on("previous", nbr, shard(7))
    ag_copies[2].wait_recv()
    pass_on(3, shard(6), shard(1))
    ag_copies[6].wait_recv()
    pass_on(5, shard(2), shard(7))
    upward = lax.rem(z + 2 + 4 * core, RING) * 2 + x
    downward = lax.rem(z + 6 - 4 * core, RING) * 2 + x
    pass_on(4, downward, upward)
    pass_on("x2", shard(6), nbr)
    pass_on("x6", shard(2), nbr)
    norm(1)
    unfold(1)
    for k in (3, 5, 4):
        ag_copies[k].wait_recv()
        pass_on("x%d" % k, shard(RING - k), nbr)
    for name in ("main", "last", "tgt", "spread"):
        inputs[name].wait()
    for name in (1, 7, "next", "previous", "x2", "x6", "x3", "x5", "x4"):
        ag_copies[name].wait_recv()
    for copy in ag_copies.values():
        copy.wait_send()

    main = got[:, :, :WIDE].reshape(512, WIDE)
    tails = jnp.concatenate([unpack_last(got[s, :, WIDE:]) for s in range(16)], axis=0)
    kernels = jnp.dot(main_ref[...], main, preferred_element_type=F32) + jnp.dot(
        last_ref[...], tails, preferred_element_type=F32
    )
    both[...] = kernels.astype(BF16).reshape(2, 288, WIDE)

    first, second = count_ref[0, 0], count_ref[0, 1]
    which = []
    grads = []
    zero = jnp.zeros((C, PLANE), F32)
    for i in range(2):
        place = f * 2 + i
        in_first = place < first
        in_second = (place >= first) & (place < first + second)
        which.append(in_second.astype(jnp.int32))
        live = jnp.where(in_first | in_second, reward_ref[i], 0.0)
        taps = jnp.dot(both[which[i]], cols[i], preferred_element_type=F32)
        mixed = (
            jnp.concatenate([zero, taps[:C, :-PLANE]], axis=1)
            + taps[C : 2 * C]
            + jnp.concatenate([taps[2 * C :, PLANE:], zero], axis=1)
        )
        upstream = live * (lat_ref[i].astype(F32) + mixed - tgt_ref[i].astype(F32))
        ups[i] = upstream
        rounded = upstream.astype(BF16)
        none = jnp.zeros((C, PLANE), BF16)
        ucat[i, :C] = jnp.concatenate([rounded[:, PLANE:], none], axis=1)
        ucat[i, C : 2 * C] = rounded
        ucat[i, 2 * C :] = jnp.concatenate([none, rounded[:, :-PLANE]], axis=1)
        grad = lax.dot_general(
            ucat[i], cols[i], (((1,), (1,)), ((), ())), preferred_element_type=F32
        )
        grads.append(
            (
                grad * (jnp.where(in_first, 1.0, 0.0) / CELLS),
                grad * (jnp.where(in_second, 1.0, 0.0) / CELLS),
            )
        )
    sums = jnp.concatenate(
        [(grads[0][j] + grads[1][j]).astype(BF16) for j in range(2)], axis=0
    )

    rs_copies = {}

    def send(name, src, at, to):
        copy = rcopy(src, landed.at[at], (rs_s, rs_r), at, {"fsdp": to})
        copy.start()
        rs_copies[name] = (copy, at)

    def arrived(name):
        copy, at = rs_copies[name]
        copy.wait_recv()
        return landed[at].astype(F32)

    def send_sum(name, k, column, terms, slot, at, to):
        value = part[2 * k + column].astype(F32)
        for term in terms:
            value = value + term
        stage[slot] = value.astype(BF16)
        send(name, stage.at[slot], at, to)

    for step in (4, 2, 6, 0):
        at = pl.multiple_of((z + step) * 80, 16)
        spread = jnp.dot(spread_ref[pl.ds(at, 160), :], sums, preferred_element_type=F32)
        for i in range(2):
            k = step + i
            for c in range(2):
                row = i * 80 + c * 40
                part[k * 2 + c] = pack(spread[row : row + 40])
            if 2 <= k <= 6:
                send("x%d" % k, part.at[k * 2 + 1 - x], k, nbr)
            elif k == 1:
                send("side1", part.at[k * 2 + 1 - x], 7, shard(1))
                send("own1", part.at[k * 2 + x], 8, shard(1))
            elif k == 7:
                send("side7", part.at[k * 2 + 1 - x], 9, shard(7))
                send("own7", part.at[k * 2 + x], 10, shard(7))

    def back(i):
        products = lax.dot_general(
            both[which[i]], ucat[i], (((0,), (0,)), ((), ())), preferred_element_type=F32
        )
        acc = products[4 * C : 5 * C]
        for at, (dy, dz) in enumerate(SHIFTS):
            move = 16 * dy + dz
            if move != 0:
                piece = products[at * C : (at + 1) * C]
                acc = acc + jnp.where(
                    inside(lane, -dy, -dz), pltpu.roll(piece, move % CELLS, 1), 0.0
                )
        fold[...] = acc

    results = []

    def finish(i):
        value = normed[i]
        flow = fold[...] * slope[i]
        start = rstd[i][:, :1] * (flow - group_mean(flow) - value * group_mean(flow * value))
        gi_ref[i] = (ups[i] + start).astype(BF16)
        result = pltpu.make_async_copy(gi_ref.at[i], gi_hbm.at[i], in_s.at[8 + i])
        result.start()
        results.append(result)

    back(0)
    send_sum("far4", 4, x, [arrived("x4")], 0, 11, upward)
    send_sum("far5", 5, x, [arrived("x5")], 1, 12, shard(7))
    send_sum("far3", 3, x, [arrived("x3")], 2, 13, shard(1))
    finish(0)
    send_sum("x0", 0, 1 - x, [arrived("side1"), arrived("side7")], 3, 0, nbr)
    back(1)
    far4 = arrived("far4")
    send_sum(
        "own2", 2, x,
        [arrived("x2"), arrived("far3"), jnp.where(core == 0, far4, 0.0)], 4, 14, shard(2),
    )
    send_sum(
        "own6", 6, x,
        [arrived("x6"), arrived("far5"), jnp.where(core == 1, far4, 0.0)], 5, 1, shard(6),
    )
    finish(1)
    lane_sum = part[x].astype(F32)
    for name in ("own1", "own7", "x0", "own2", "own6"):
        lane_sum = lane_sum + arrived(name)
    lane_sum = lane_sum.astype(BF16)
    lane_out[...] = jnp.concatenate(
        [lane_sum[:, :WIDE], unpack_last(lane_sum[:, WIDE:])], axis=0
    )

    dp = (dp_s, dp_r)
    own_half = OUT_TILES // 2
    share = own_half // chips
    first_tile = core * own_half
    pair = rcopy(lane_out, lane_in, dp, 30, {"dp": twin})
    pair.start()
    wide = jnp.dot(choose_out[...], lane_out[...], preferred_element_type=F32)
    told.wait_recv()
    pair.wait_recv()
    wide = wide + jnp.dot(choose_in[...], lane_in[...], preferred_element_type=F32)
    wide = wide.astype(BF16)
    for r in range(9):
        for t in range(TILES):
            table[r * TILES + t] = wide[r * 16 : (r + 1) * 16, t * 128 : (t + 1) * 128]
    table[OUT_TILES - 1] = jnp.zeros((16, 128), BF16)

    scatters = []
    for i, peer in enumerate(peers):
        copy = rcopy(
            table.at[pl.ds(first_tile + peer * share, share)], chunk_in.at[i], dp, i,
            {"dp": peer * 2 + core},
        )
        copy.start()
        scatters.append(copy)
    own = pl.ds(first_tile + chip * share, share)
    acc = table[own].astype(F32)
    for i, copy in enumerate(scatters):
        copy.wait_recv()
        acc = acc + chunk_in[i].astype(F32)
    full[own] = acc.astype(BF16)
    gathers = []
    for i, peer in enumerate(peers):
        copy = rcopy(full.at[own], full.at[own], dp, 15 + i, {"dp": peer * 2 + core})
        copy.start()
        gathers.append(copy)
    for copy in gathers:
        copy.wait_recv()
    mine = pl.ds(first_tile, own_half)
    last = rcopy(full.at[mine], full.at[mine], dp, 31, {"dp": twin})
    last.start()
    last.wait_recv()
    for copy in results:
        copy.wait()
    for copy in [copy for copy, _ in rs_copies.values()] + [pair, told, last] + scatters + gathers:
        copy.wait_send()


def finish_kernel(full, gi_in, gw_ref, gi_out, gi_ref, sem):
    move = pltpu.make_async_copy(gi_in, gi_ref, sem.at[0])
    move.start()
    move.wait()
    move = pltpu.make_async_copy(gi_ref, gi_out, sem.at[1])
    move.start()
    for dx in range(3):
        for r in range(6):
            at = dx * 6 + r
            line = jnp.concatenate(
                [full[at // 2 * TILES + t].astype(F32)[at % 2 * 8 :][:8] for t in range(TILES)],
                axis=1,
            )
            gw_ref[r, :, dx * SPAN : (dx + 1) * SPAN] = line[:, :SPAN]
    move.wait()


def local(
    chips,
    latents,
    targets,
    rewards,
    time_steps,
    time_table,
    norm_gain,
    norm_bias,
    expert_weights,
    lane_experts,
    lane_counts,
):
    main, last, spread, group = constants()
    vmem = pl.BlockSpec(memory_space=pltpu.VMEM)
    smem = pl.BlockSpec(memory_space=pltpu.SMEM)
    sems = pltpu.SemaphoreType.DMA
    hbm = pl.BlockSpec(memory_space=pltpu.MemorySpace.HBM)
    full, grad_input = pl.pallas_call(
        functools.partial(kernel, chips),
        out_shape=(
            jax.ShapeDtypeStruct((OUT_TILES, 16, 128), BF16),
            jax.ShapeDtypeStruct((2, C, CELLS), BF16),
        ),
        in_specs=[hbm, hbm, smem, smem, hbm, vmem, vmem, hbm, smem, smem] + [hbm] * 4,
        out_specs=(vmem, hbm),
        scratch_shapes=[
            pltpu.VMEM((2, C, CELLS), BF16),
            pltpu.VMEM((48, 3 * SPAN), BF16),
            pltpu.VMEM((2, C, CELLS), BF16),
            pltpu.VMEM((2, C, CELLS), BF16),
            pltpu.VMEM(time_table.shape[::-1], F32),
            pltpu.VMEM(main.shape, BF16),
            pltpu.VMEM(last.shape, BF16),
            pltpu.VMEM(spread.shape, BF16),
            pltpu.VMEM(group.shape, F32),
            pltpu.VMEM((16,) + PACK, BF16),
            pltpu.VMEM((2, C, CELLS), F32),
            pltpu.VMEM((2, C, CELLS), F32),
            pltpu.VMEM((2, C, 128), F32),
            pltpu.VMEM((2, WIDE, CELLS), BF16),
            pltpu.VMEM((2, 288, WIDE), BF16),
            pltpu.VMEM((2, C, CELLS), F32),
            pltpu.VMEM((2, 288, CELLS), BF16),
            pltpu.VMEM((C, CELLS), F32),
            pltpu.VMEM((16,) + PACK, BF16),
            pltpu.VMEM((15,) + PACK, BF16),
            pltpu.VMEM((6,) + PACK, BF16),
            pltpu.VMEM((144, BLOCK), BF16),
            pltpu.VMEM((144, BLOCK), BF16),
            pltpu.VMEM((BLOCK, WIDE), BF16),
            pltpu.VMEM((BLOCK, WIDE), BF16),
            pltpu.VMEM((OUT_TILES, 16, 128), BF16),
            pltpu.VMEM((15, OUT_TILES // 2 // chips, 16, 128), BF16),
            sems((15,)),
            sems((15,)),
            sems((15,)),
            sems((15,)),
            sems((33,)),
            sems((33,)),
            sems((10,)),
        ],
        compiler_params=pltpu.CompilerParams(
            collective_id=0, has_side_effects=True, vmem_limit_bytes=60 * 2**20
        ),
    )(
        latents, targets, rewards, time_steps, time_table.T, norm_gain[None, :],
        norm_bias[None, :], expert_weights.swapaxes(0, 1).reshape(48, 3 * SPAN), lane_experts,
        lane_counts,
        jnp.asarray(main, BF16), jnp.asarray(last, BF16), jnp.asarray(spread, BF16),
        jnp.asarray(group, F32),
    )
    grad_weight, grad_input = pl.pallas_call(
        finish_kernel,
        out_shape=(
            jax.ShapeDtypeStruct((6, 8, 3 * SPAN), F32),
            jax.ShapeDtypeStruct((2, C, CELLS), BF16),
        ),
        in_specs=[vmem, hbm],
        out_specs=(vmem, hbm),
        scratch_shapes=[pltpu.VMEM((2, C, CELLS), BF16), sems((2,))],
    )(full, grad_input)
    return grad_weight.swapaxes(0, 1), grad_input


def solution(mesh):
    placed = (
        P(("dp", "fsdp"), None, None),
        P(("dp", "fsdp"), None, None),
        P(("dp", "fsdp")),
        P(("dp", "fsdp")),
        P(),
        P(),
        P(),
        P(None, "fsdp", None),
        P("dp", None),
        P("dp", None),
    )
    return jax.shard_map(
        functools.partial(local, mesh.shape["dp"] // 2),
        mesh=mesh,
        in_specs=placed,
        out_specs=(P(None, "fsdp", None), P(("dp", "fsdp"), None, None)),
        check_vma=False,
    )
```

```python
import functools

import jax
import jax.numpy as jnp
import numpy as np
from jax import lax
from jax.experimental import pallas as pl
from jax.experimental.pallas import tpu as pltpu
from jax.sharding import PartitionSpec as P

GROUPS = 32
SIDE = 16
DEPTH = 4
EPSILON = 1e-05
MESH = pl.DeviceIdType.MESH
RING = 8
C = 96
CELLS = 1024
PLANE = SIDE * SIDE
SPAN = 864
WIDE = 896
TILES = WIDE // 128
ROWS = 36
PACK = (32, WIDE + 128)
BLOCK = 48
OUT_TILES = 64
SHIFTS = [(dy, dz) for dy in (-1, 0, 1) for dz in (-1, 0, 1)]
F32 = jnp.float32
BF16 = jnp.bfloat16


def constants():
    main = np.zeros((576, 512), np.float32)
    last = np.zeros((576, 256), np.float32)
    spread = np.zeros((16 * 40, 576), np.float32)
    for s in range(16):
        for q in range(ROWS):
            dx, j, r = q // 12, q % 12 // 6, q % 6
            row = j * 288 + dx * C + 6 * s + r
            if q < 32:
                main[row, 32 * s + q] = 1
            else:
                last[row, 16 * s + q - 32] = 1
                spread[40 * s + q + 4, row] = 1
            spread[40 * s + q, row] = 1
    group = np.kron(np.eye(GROUPS, dtype=np.float32), np.ones((3, 3), np.float32))
    return main, last, np.concatenate([spread, spread]), group


def rcopy(src, dst, sems, at, device_id):
    return pltpu.make_async_remote_copy(
        src_ref=src,
        dst_ref=dst,
        send_sem=sems[0].at[at],
        recv_sem=sems[1].at[at],
        device_id=device_id,
        device_id_type=MESH,
    )


def column_of(row, eye):
    return jnp.sum(eye * row, axis=1, keepdims=True)


def inside(lane, dy, dz):
    row = lane // SIDE % SIDE
    col = lane % SIDE
    ok = None
    for at, step in ((row, dy), (col, dz)):
        if step != 0:
            one = (at + step >= 0) & (at + step < SIDE)
            ok = one if ok is None else ok & one
    return ok


def pack(rows40):
    half = lax.broadcasted_iota(jnp.int32, (8, 128), 0) < 4
    tail = [rows40[32:40, t * 128 : (t + 1) * 128] for t in range(TILES)] + [
        jnp.zeros((8, 128), F32)
    ]
    last = [jnp.where(half, tail[t], tail[t + 1]) for t in range(0, 8, 2)]
    packed = jnp.concatenate([rows40[:32], jnp.concatenate(last, axis=0)], axis=1)
    return packed.astype(BF16)


def unpack_last(last):
    last = last.astype(F32)
    keep = lax.broadcasted_iota(jnp.int32, (16, 128), 0) < 4
    pieces = []
    for t in range(TILES):
        rolled = last if t == 0 else pltpu.roll(last, 32 - 4 * t, 0)
        pieces.append(jnp.where(keep, rolled[:16], 0.0))
    return jnp.concatenate(pieces, axis=1).astype(BF16)


def kernel(
    chips,
    lat_hbm, tgt_hbm, reward_hbm, step_hbm, time_hbm, gain_hbm, bias_hbm, weight_hbm, pair_hbm,
    count_hbm, main_hbm, last_hbm, spread_hbm, group_hbm,
    full, gi_hbm,
    reward_ref, step_ref, gain_ref, bias_ref, pair_ref, count_ref, gi_ref, weight_ref, lat_ref, tgt_ref, time_ref, main_ref, last_ref, spread_ref, group_ref,
    got, normed, slope, rstd, cols, both, ups, ucat, fold, part, landed, stage,
    choose_out, choose_in, lane_out, lane_in, table, chunk_in,
    ag_s, ag_r, rs_s, rs_r, dp_s, dp_r, in_s,
):
    f = lax.axis_index("fsdp")
    z = f // 2
    x = f % 2
    nbr = z * 2 + 1 - x
    d = lax.axis_index("dp")
    core = d % 2
    chip = d // 2
    twin = chip * 2 + 1 - core
    peers = [lax.rem(chip + i, chips) for i in range(1, chips)]
    ring = {k: lax.rem(z + k, RING) for k in range(RING)}
    barrier = pltpu.get_barrier_semaphore()
    for other in [nbr] + [ring[k] * 2 + x for k in (1, 7, 2, 6)]:
        pl.semaphore_signal(barrier, inc=1, device_id={"fsdp": other}, device_id_type=MESH)
    pl.semaphore_signal(barrier, inc=1, device_id={"dp": twin}, device_id_type=MESH)
    for peer in peers:
        pl.semaphore_signal(
            barrier, inc=1, device_id={"dp": peer * 2 + core}, device_id_type=MESH
        )
    inputs = {}
    for at, (name, src, dst) in enumerate((
        ("pair", pair_hbm, pair_ref), ("weight", weight_hbm, weight_ref),
        ("step", step_hbm, step_ref), ("gain", gain_hbm, gain_ref), ("bias", bias_hbm, bias_ref),
        ("count", count_hbm, count_ref), ("reward", reward_hbm, reward_ref), ("lat", lat_hbm, lat_ref),
        ("time", time_hbm, time_ref), ("group", group_hbm, group_ref),
        ("main", main_hbm, main_ref), ("last", last_hbm, last_ref), ("tgt", tgt_hbm, tgt_ref),
        ("spread", spread_hbm, spread_ref),
    )):
        inputs[name] = pltpu.make_async_copy(src, dst, in_s.at[at])
        inputs[name].start()

    inputs["pair"].wait()
    row = lax.broadcasted_iota(jnp.int32, (16, 48), 0)
    col = lax.broadcasted_iota(jnp.int32, (16, 48), 1)
    expert = jnp.where(row < 6, pair_ref[0, 0], pair_ref[0, 1] - 48)
    pick = ((col - 8 * row == expert) & (row < 12)).astype(F32).astype(BF16)
    inputs["weight"].wait()
    mine = jnp.dot(pick, weight_ref[...], preferred_element_type=F32)[:12]
    rows = [mine[:, dx * SPAN : (dx + 1) * SPAN] for dx in range(3)]
    rows.append(rows[2][8:12])
    stacked = jnp.concatenate(rows, axis=0)
    stacked = jnp.concatenate([stacked, jnp.zeros((40, WIDE - SPAN), F32)], axis=1)
    got[f] = pack(stacked)
    pl.semaphore_wait(barrier, 6 + len(peers))

    row = lax.broadcasted_iota(jnp.int32, (144, BLOCK), 0)
    col = lax.broadcasted_iota(jnp.int32, (144, BLOCK), 1)
    expert = jnp.where(col % 12 < 6, pair_ref[0, 0], pair_ref[0, 1])
    choose_out[...] = (
        (row // 48 == col // 12) & (row % 48 // 8 == col % 6) & (row % 8 == expert)
    ).astype(F32).astype(BF16)

    ag_copies = {}

    def pass_on(name, item, to):
        at = len(ag_copies)
        copy = rcopy(got.at[item], got.at[item], (ag_s, ag_r), at, {"fsdp": to})
        copy.start()
        ag_copies[name] = copy

    def shard(k):
        return ring[k] * 2 + x

    pass_on("swap", f, nbr)
    for k in (2, 6, 1, 7):
        pass_on(k, f, shard(k))
    told = rcopy(choose_out, choose_in, (dp_s, dp_r), 32, {"dp": twin})
    told.start()

    eye = (
        lax.broadcasted_iota(jnp.int32, (C, C), 0) == lax.broadcasted_iota(jnp.int32, (C, C), 1)
    ).astype(F32)
    for name in ("step", "gain", "bias", "count", "reward"):
        inputs[name].wait()
    gain = column_of(gain_ref[...], eye)
    bias = column_of(bias_ref[...], eye)
    lane = lax.broadcasted_iota(jnp.int32, (C, CELLS), 1)
    moment = lax.broadcasted_iota(jnp.int32, time_ref.shape, 1)

    def group_mean(field):
        sums = jnp.broadcast_to(jnp.sum(field, axis=1, keepdims=True), (C, 128))
        spread = jnp.dot(
            group_ref[...], sums, precision=lax.Precision.HIGHEST, preferred_element_type=F32
        )
        return spread[:, :1] * (1.0 / (3 * CELLS))

    def norm(i):
        start = lat_ref[i].astype(F32) + jnp.sum(
            jnp.where(moment == step_ref[i], time_ref[...], 0.0), axis=1, keepdims=True
        )
        centred = start - group_mean(start)
        scale = lax.rsqrt(group_mean(centred * centred) + EPSILON)
        value = centred * scale
        pre = value * gain + bias
        sig = 1.0 / (1.0 + jnp.exp(-pre))
        normed[i] = value
        slope[i] = sig * (1.0 + pre * (1.0 - sig)) * gain
        rstd[i] = jnp.broadcast_to(scale, (C, 128))
        fold[...] = (pre * sig).astype(BF16).astype(F32)

    def unfold(i):
        act = fold[...]
        for at, (dy, dz) in enumerate(SHIFTS):
            move = 16 * dy + dz
            value = act
            if move != 0:
                value = jnp.where(
                    inside(lane, dy, dz), pltpu.roll(act, (-move) % CELLS, 1), 0.0
                )
            cols[i, at * C : (at + 1) * C, :] = value.astype(BF16)
        cols[i, SPAN:WIDE, :] = jnp.zeros((WIDE - SPAN, CELLS), BF16)

    for name in ("lat", "time", "group"):
        inputs[name].wait()
    norm(0)
    unfold(0)
    ag_copies["swap"].wait_recv()
    pass_on("next", nbr, shard(1))
    pass_on("previous", nbr, shard(7))
    ag_copies[2].wait_recv()
    pass_on(3, shard(6), shard(1))
    ag_copies[6].wait_recv()
    pass_on(5, shard(2), shard(7))
    upward = lax.rem(z + 2 + 4 * core, RING) * 2 + x
    downward = lax.rem(z + 6 - 4 * core, RING) * 2 + x
    pass_on(4, downward, upward)
    pass_on("x2", shard(6), nbr)
    pass_on("x6", shard(2), nbr)
    norm(1)
    unfold(1)
    for k in (3, 5, 4):
        ag_copies[k].wait_recv()
        pass_on("x%d" % k, shard(RING - k), nbr)
    for name in ("main", "last", "tgt", "spread"):
        inputs[name].wait()
    for name in (1, 7, "next", "previous", "x2", "x6", "x3", "x5", "x4"):
        ag_copies[name].wait_recv()
    for copy in ag_copies.values():
        copy.wait_send()

    main = got[:, :, :WIDE].reshape(512, WIDE)
    tails = jnp.concatenate([unpack_last(got[s, :, WIDE:]) for s in range(16)], axis=0)
    kernels = jnp.dot(main_ref[...], main, preferred_element_type=F32) + jnp.dot(
        last_ref[...], tails, preferred_element_type=F32
    )
    both[...] = kernels.astype(BF16).reshape(2, 288, WIDE)

    first, second = count_ref[0, 0], count_ref[0, 1]
    which = []
    grads = []
    zero = jnp.zeros((C, PLANE), F32)
    for i in range(2):
        place = f * 2 + i
        in_first = place < first
        in_second = (place >= first) & (place < first + second)
        which.append(in_second.astype(jnp.int32))
        live = jnp.where(in_first | in_second, reward_ref[i], 0.0)
        taps = jnp.dot(both[which[i]], cols[i], preferred_element_type=F32)
        mixed = (
            jnp.concatenate([zero, taps[:C, :-PLANE]], axis=1)
            + taps[C : 2 * C]
            + jnp.concatenate([taps[2 * C :, PLANE:], zero], axis=1)
        )
        upstream = live * (lat_ref[i].astype(F32) + mixed - tgt_ref[i].astype(F32))
        ups[i] = upstream
        rounded = upstream.astype(BF16)
        none = jnp.zeros((C, PLANE), BF16)
        ucat[i, :C] = jnp.concatenate([rounded[:, PLANE:], none], axis=1)
        ucat[i, C : 2 * C] = rounded
        ucat[i, 2 * C :] = jnp.concatenate([none, rounded[:, :-PLANE]], axis=1)
        grad = lax.dot_general(
            ucat[i], cols[i], (((1,), (1,)), ((), ())), preferred_element_type=F32
        )
        grads.append(
            (
                grad * (jnp.where(in_first, 1.0, 0.0) / CELLS),
                grad * (jnp.where(in_second, 1.0, 0.0) / CELLS),
            )
        )
    sums = jnp.concatenate(
        [(grads[0][j] + grads[1][j]).astype(BF16) for j in range(2)], axis=0
    )

    rs_copies = {}

    def send(name, src, at, to):
        copy = rcopy(src, landed.at[at], (rs_s, rs_r), at, {"fsdp": to})
        copy.start()
        rs_copies[name] = (copy, at)

    def arrived(name):
        copy, at = rs_copies[name]
        copy.wait_recv()
        return landed[at].astype(F32)

    def send_sum(name, k, column, terms, slot, at, to):
        value = part[2 * k + column].astype(F32)
        for term in terms:
            value = value + term
        stage[slot] = value.astype(BF16)
        send(name, stage.at[slot], at, to)

    for step in (4, 2, 6, 0):
        at = pl.multiple_of((z + step) * 80, 16)
        spread = jnp.dot(spread_ref[pl.ds(at, 160), :], sums, preferred_element_type=F32)
        for i in range(2):
            k = step + i
            for c in range(2):
                row = i * 80 + c * 40
                part[k * 2 + c] = pack(spread[row : row + 40])
            if 2 <= k <= 6:
                send("x%d" % k, part.at[k * 2 + 1 - x], k, nbr)
            elif k == 1:
                send("side1", part.at[k * 2 + 1 - x], 7, shard(1))
                send("own1", part.at[k * 2 + x], 8, shard(1))
            elif k == 7:
                send("side7", part.at[k * 2 + 1 - x], 9, shard(7))
                send("own7", part.at[k * 2 + x], 10, shard(7))

    def back(i):
        products = lax.dot_general(
            both[which[i]], ucat[i], (((0,), (0,)), ((), ())), preferred_element_type=F32
        )
        acc = products[4 * C : 5 * C]
        for at, (dy, dz) in enumerate(SHIFTS):
            move = 16 * dy + dz
            if move != 0:
                piece = products[at * C : (at + 1) * C]
                acc = acc + jnp.where(
                    inside(lane, -dy, -dz), pltpu.roll(piece, move % CELLS, 1), 0.0
                )
        fold[...] = acc

    results = []

    def finish(i):
        value = normed[i]
        flow = fold[...] * slope[i]
        start = rstd[i][:, :1] * (flow - group_mean(flow) - value * group_mean(flow * value))
        gi_ref[i] = (ups[i] + start).astype(BF16)
        result = pltpu.make_async_copy(gi_ref.at[i], gi_hbm.at[i], in_s.at[14 + i])
        result.start()
        results.append(result)

    back(0)
    send_sum("far4", 4, x, [arrived("x4")], 0, 11, upward)
    send_sum("far5", 5, x, [arrived("x5")], 1, 12, shard(7))
    send_sum("far3", 3, x, [arrived("x3")], 2, 13, shard(1))
    finish(0)
    send_sum("x0", 0, 1 - x, [arrived("side1"), arrived("side7")], 3, 0, nbr)
    back(1)
    far4 = arrived("far4")
    send_sum(
        "own2", 2, x,
        [arrived("x2"), arrived("far3"), jnp.where(core == 0, far4, 0.0)], 4, 14, shard(2),
    )
    send_sum(
        "own6", 6, x,
        [arrived("x6"), arrived("far5"), jnp.where(core == 1, far4, 0.0)], 5, 1, shard(6),
    )
    finish(1)
    lane_sum = part[x].astype(F32)
    for name in ("own1", "own7", "x0", "own2", "own6"):
        lane_sum = lane_sum + arrived(name)
    lane_sum = lane_sum.astype(BF16)
    lane_out[...] = jnp.concatenate(
        [lane_sum[:, :WIDE], unpack_last(lane_sum[:, WIDE:])], axis=0
    )

    dp = (dp_s, dp_r)
    own_half = OUT_TILES // 2
    share = own_half // chips
    first_tile = core * own_half
    pair = rcopy(lane_out, lane_in, dp, 30, {"dp": twin})
    pair.start()
    wide = jnp.dot(choose_out[...], lane_out[...], preferred_element_type=F32)
    told.wait_recv()
    pair.wait_recv()
    wide = wide + jnp.dot(choose_in[...], lane_in[...], preferred_element_type=F32)
    wide = wide.astype(BF16)
    for r in range(9):
        for t in range(TILES):
            table[r * TILES + t] = wide[r * 16 : (r + 1) * 16, t * 128 : (t + 1) * 128]
    table[OUT_TILES - 1] = jnp.zeros((16, 128), BF16)

    scatters = []
    for i, peer in enumerate(peers):
        copy = rcopy(
            table.at[pl.ds(first_tile + peer * share, share)], chunk_in.at[i], dp, i,
            {"dp": peer * 2 + core},
        )
        copy.start()
        scatters.append(copy)
    own = pl.ds(first_tile + chip * share, share)
    acc = table[own].astype(F32)
    for i, copy in enumerate(scatters):
        copy.wait_recv()
        acc = acc + chunk_in[i].astype(F32)
    full[own] = acc.astype(BF16)
    gathers = []
    for i, peer in enumerate(peers):
        copy = rcopy(full.at[own], full.at[own], dp, 15 + i, {"dp": peer * 2 + core})
        copy.start()
        gathers.append(copy)
    for copy in gathers:
        copy.wait_recv()
    mine = pl.ds(first_tile, own_half)
    last = rcopy(full.at[mine], full.at[mine], dp, 31, {"dp": twin})
    last.start()
    last.wait_recv()
    for copy in results:
        copy.wait()
    for copy in [copy for copy, _ in rs_copies.values()] + [pair, told, last] + scatters + gathers:
        copy.wait_send()


def finish_kernel(full_hbm, gi_in, gw_hbm, gi_out, full, gi_ref, gw_ref, sem):
    moves = [
        pltpu.make_async_copy(full_hbm, full, sem.at[0]),
        pltpu.make_async_copy(gi_in, gi_ref, sem.at[1]),
    ]
    for move in moves:
        move.start()
    for move in moves:
        move.wait()
    moves = [pltpu.make_async_copy(gi_ref, gi_out, sem.at[2])]
    moves[0].start()
    for r in range(6):
        for dx in range(3):
            at = dx * 6 + r
            line = jnp.concatenate(
                [full[at // 2 * TILES + t].astype(F32)[at % 2 * 8 :][:8] for t in range(TILES)],
                axis=1,
            )
            gw_ref[r, :, dx * SPAN : (dx + 1) * SPAN] = line[:, :SPAN]
        move = pltpu.make_async_copy(gw_ref.at[r], gw_hbm.at[r], sem.at[3 + r])
        move.start()
        moves.append(move)
    for move in moves:
        move.wait()


def local(
    chips,
    latents,
    targets,
    rewards,
    time_steps,
    time_table,
    norm_gain,
    norm_bias,
    expert_weights,
    lane_experts,
    lane_counts,
):
    main, last, spread, group = constants()
    vmem = pl.BlockSpec(memory_space=pltpu.VMEM)
    smem = pltpu.MemorySpace.SMEM
    sems = pltpu.SemaphoreType.DMA
    hbm = pl.BlockSpec(memory_space=pltpu.MemorySpace.HBM)
    full, grad_input = pl.pallas_call(
        functools.partial(kernel, chips),
        out_shape=(
            jax.ShapeDtypeStruct((OUT_TILES, 16, 128), BF16),
            jax.ShapeDtypeStruct((2, C, CELLS), BF16),
        ),
        in_specs=[hbm] * 14,
        out_specs=(vmem, hbm),
        scratch_shapes=[
            smem((2,), F32),
            smem((2,), jnp.int32),
            pltpu.VMEM((1, C), F32),
            pltpu.VMEM((1, C), F32),
            smem((1, 2), jnp.int32),
            smem((1, 2), jnp.int32),
            pltpu.VMEM((2, C, CELLS), BF16),
            pltpu.VMEM((48, 3 * SPAN), BF16),
            pltpu.VMEM((2, C, CELLS), BF16),
            pltpu.VMEM((2, C, CELLS), BF16),
            pltpu.VMEM(time_table.shape[::-1], F32),
            pltpu.VMEM(main.shape, BF16),
            pltpu.VMEM(last.shape, BF16),
            pltpu.VMEM(spread.shape, BF16),
            pltpu.VMEM(group.shape, F32),
            pltpu.VMEM((16,) + PACK, BF16),
            pltpu.VMEM((2, C, CELLS), F32),
            pltpu.VMEM((2, C, CELLS), F32),
            pltpu.VMEM((2, C, 128), F32),
            pltpu.VMEM((2, WIDE, CELLS), BF16),
            pltpu.VMEM((2, 288, WIDE), BF16),
            pltpu.VMEM((2, C, CELLS), F32),
            pltpu.VMEM((2, 288, CELLS), BF16),
            pltpu.VMEM((C, CELLS), F32),
            pltpu.VMEM((16,) + PACK, BF16),
            pltpu.VMEM((15,) + PACK, BF16),
            pltpu.VMEM((6,) + PACK, BF16),
            pltpu.VMEM((144, BLOCK), BF16),
            pltpu.VMEM((144, BLOCK), BF16),
            pltpu.VMEM((BLOCK, WIDE), BF16),
            pltpu.VMEM((BLOCK, WIDE), BF16),
            pltpu.VMEM((OUT_TILES, 16, 128), BF16),
            pltpu.VMEM((15, OUT_TILES // 2 // chips, 16, 128), BF16),
            sems((15,)),
            sems((15,)),
            sems((15,)),
            sems((15,)),
            sems((33,)),
            sems((33,)),
            sems((16,)),
        ],
        compiler_params=pltpu.CompilerParams(
            collective_id=0, has_side_effects=True, vmem_limit_bytes=60 * 2**20
        ),
    )(
        latents, targets, rewards, time_steps, time_table.T, norm_gain[None, :],
        norm_bias[None, :], expert_weights.swapaxes(0, 1).reshape(48, 3 * SPAN), lane_experts,
        lane_counts,
        jnp.asarray(main, BF16), jnp.asarray(last, BF16), jnp.asarray(spread, BF16),
        jnp.asarray(group, F32),
    )
    grad_weight, grad_input = pl.pallas_call(
        finish_kernel,
        out_shape=(
            jax.ShapeDtypeStruct((6, 8, 3 * SPAN), F32),
            jax.ShapeDtypeStruct((2, C, CELLS), BF16),
        ),
        in_specs=[hbm, hbm],
        out_specs=(hbm, hbm),
        scratch_shapes=[
            pltpu.VMEM((OUT_TILES, 16, 128), BF16),
            pltpu.VMEM((2, C, CELLS), BF16),
            pltpu.VMEM((6, 8, 3 * SPAN), F32),
            sems((9,)),
        ],
    )(full, grad_input)
    return grad_weight.swapaxes(0, 1), grad_input


def solution(mesh):
    placed = (
        P(("dp", "fsdp"), None, None),
        P(("dp", "fsdp"), None, None),
        P(("dp", "fsdp")),
        P(("dp", "fsdp")),
        P(),
        P(),
        P(),
        P(None, "fsdp", None),
        P("dp", None),
        P("dp", None),
    )
    return jax.shard_map(
        functools.partial(local, mesh.shape["dp"] // 2),
        mesh=mesh,
        in_specs=placed,
        out_specs=(P(None, "fsdp", None), P(("dp", "fsdp"), None, None)),
        check_vma=False,
    )
```

```python
import functools

import jax
import jax.numpy as jnp
import numpy as np
from jax import lax
from jax.experimental import pallas as pl
from jax.experimental.pallas import tpu as pltpu
from jax.sharding import PartitionSpec as P

GROUPS = 32
SIDE = 16
DEPTH = 4
EPSILON = 1e-05
MESH = pl.DeviceIdType.MESH
RING = 8
C = 96
CELLS = 1024
PLANE = SIDE * SIDE
SPAN = 864
WIDE = 896
TILES = WIDE // 128
ROWS = 36
PACK = (32, WIDE + 128)
BLOCK = 48
OUT_TILES = 64
SHIFTS = [(dy, dz) for dy in (-1, 0, 1) for dz in (-1, 0, 1)]
F32 = jnp.float32
BF16 = jnp.bfloat16


def constants():
    main = np.zeros((576, 512), np.float32)
    last = np.zeros((576, 256), np.float32)
    spread = np.zeros((16 * 40, 576), np.float32)
    for s in range(16):
        for q in range(ROWS):
            dx, j, r = q // 12, q % 12 // 6, q % 6
            row = j * 288 + dx * C + 6 * s + r
            if q < 32:
                main[row, 32 * s + q] = 1
            else:
                last[row, 16 * s + q - 32] = 1
                spread[40 * s + q + 4, row] = 1
            spread[40 * s + q, row] = 1
    group = np.kron(np.eye(GROUPS, dtype=np.float32), np.ones((3, 3), np.float32))
    return main, last, np.concatenate([spread, spread]), group


def rcopy(src, dst, sems, at, device_id):
    return pltpu.make_async_remote_copy(
        src_ref=src,
        dst_ref=dst,
        send_sem=sems[0].at[at],
        recv_sem=sems[1].at[at],
        device_id=device_id,
        device_id_type=MESH,
    )


def column_of(row, eye):
    return jnp.sum(eye * row, axis=1, keepdims=True)


def inside(lane, dy, dz):
    row = lane // SIDE % SIDE
    col = lane % SIDE
    ok = None
    for at, step in ((row, dy), (col, dz)):
        if step != 0:
            one = (at + step >= 0) & (at + step < SIDE)
            ok = one if ok is None else ok & one
    return ok


def pack(rows40):
    half = lax.broadcasted_iota(jnp.int32, (8, 128), 0) < 4
    tail = [rows40[32:40, t * 128 : (t + 1) * 128] for t in range(TILES)] + [
        jnp.zeros((8, 128), F32)
    ]
    last = [jnp.where(half, tail[t], tail[t + 1]) for t in range(0, 8, 2)]
    packed = jnp.concatenate([rows40[:32], jnp.concatenate(last, axis=0)], axis=1)
    return packed.astype(BF16)


def unpack_last(last):
    last = last.astype(F32)
    keep = lax.broadcasted_iota(jnp.int32, (16, 128), 0) < 4
    pieces = []
    for t in range(TILES):
        rolled = last if t == 0 else pltpu.roll(last, 32 - 4 * t, 0)
        pieces.append(jnp.where(keep, rolled[:16], 0.0))
    return jnp.concatenate(pieces, axis=1).astype(BF16)


def kernel(
    chips,
    lat_hbm, tgt_hbm, reward_hbm, step_hbm, time_hbm, gain_hbm, bias_hbm, weight_hbm, pair_hbm,
    count_hbm, main_hbm, last_hbm, spread_hbm, group_hbm,
    full, gi_hbm,
    reward_ref, step_ref, gain_ref, bias_ref, pair_ref, count_ref, gi_ref, weight_ref, lat_ref, tgt_ref, time_ref, main_ref, last_ref, spread_ref, group_ref,
    got, normed, slope, rstd, cols, both, ups, ucat, fold, part, landed, stage,
    choose_out, choose_in, lane_out, lane_in, table, chunk_in,
    ag_s, ag_r, rs_s, rs_r, dp_s, dp_r, in_s,
):
    f = lax.axis_index("fsdp")
    z = f // 2
    x = f % 2
    nbr = z * 2 + 1 - x
    d = lax.axis_index("dp")
    core = d % 2
    chip = d // 2
    twin = chip * 2 + 1 - core
    farthest = sorted(range(1, chips), key=lambda i: -min(i % 8, 8 - i % 8))
    peers = [lax.rem(chip + i, chips) for i in farthest]
    ring = {k: lax.rem(z + k, RING) for k in range(RING)}
    barrier = pltpu.get_barrier_semaphore()
    for other in [nbr] + [ring[k] * 2 + x for k in (1, 7, 2, 6)]:
        pl.semaphore_signal(barrier, inc=1, device_id={"fsdp": other}, device_id_type=MESH)
    pl.semaphore_signal(barrier, inc=1, device_id={"dp": twin}, device_id_type=MESH)
    for peer in peers:
        pl.semaphore_signal(
            barrier, inc=1, device_id={"dp": peer * 2 + core}, device_id_type=MESH
        )
    inputs = {}
    for at, (name, src, dst) in enumerate((
        ("pair", pair_hbm, pair_ref), ("weight", weight_hbm, weight_ref),
        ("step", step_hbm, step_ref), ("gain", gain_hbm, gain_ref), ("bias", bias_hbm, bias_ref),
        ("count", count_hbm, count_ref), ("reward", reward_hbm, reward_ref), ("lat", lat_hbm, lat_ref),
        ("time", time_hbm, time_ref), ("group", group_hbm, group_ref),
        ("main", main_hbm, main_ref), ("last", last_hbm, last_ref), ("tgt", tgt_hbm, tgt_ref),
        ("spread", spread_hbm, spread_ref),
    )):
        inputs[name] = pltpu.make_async_copy(src, dst, in_s.at[at])
        inputs[name].start()

    inputs["pair"].wait()
    row = lax.broadcasted_iota(jnp.int32, (16, 48), 0)
    col = lax.broadcasted_iota(jnp.int32, (16, 48), 1)
    expert = jnp.where(row < 6, pair_ref[0, 0], pair_ref[0, 1] - 48)
    pick = ((col - 8 * row == expert) & (row < 12)).astype(F32).astype(BF16)
    inputs["weight"].wait()
    mine = jnp.dot(pick, weight_ref[...], preferred_element_type=F32)[:12]
    rows = [mine[:, dx * SPAN : (dx + 1) * SPAN] for dx in range(3)]
    rows.append(rows[2][8:12])
    stacked = jnp.concatenate(rows, axis=0)
    stacked = jnp.concatenate([stacked, jnp.zeros((40, WIDE - SPAN), F32)], axis=1)
    got[f] = pack(stacked)
    pl.semaphore_wait(barrier, 6 + len(peers))

    ag_copies = {}

    def pass_on(name, item, to):
        at = len(ag_copies)
        copy = rcopy(got.at[item], got.at[item], (ag_s, ag_r), at, {"fsdp": to})
        copy.start()
        ag_copies[name] = copy

    def shard(k):
        return ring[k] * 2 + x

    pass_on("swap", f, nbr)
    for k in (2, 6, 1, 7):
        pass_on(k, f, shard(k))
    row = lax.broadcasted_iota(jnp.int32, (144, BLOCK), 0)
    col = lax.broadcasted_iota(jnp.int32, (144, BLOCK), 1)
    expert = jnp.where(col % 12 < 6, pair_ref[0, 0], pair_ref[0, 1])
    choose_out[...] = (
        (row // 48 == col // 12) & (row % 48 // 8 == col % 6) & (row % 8 == expert)
    ).astype(F32).astype(BF16)
    told = rcopy(choose_out, choose_in, (dp_s, dp_r), 32, {"dp": twin})
    told.start()

    eye = (
        lax.broadcasted_iota(jnp.int32, (C, C), 0) == lax.broadcasted_iota(jnp.int32, (C, C), 1)
    ).astype(F32)
    for name in ("step", "gain", "bias", "count", "reward"):
        inputs[name].wait()
    gain = column_of(gain_ref[...], eye)
    bias = column_of(bias_ref[...], eye)
    lane = lax.broadcasted_iota(jnp.int32, (C, CELLS), 1)
    moment = lax.broadcasted_iota(jnp.int32, time_ref.shape, 1)

    def group_mean(field):
        sums = jnp.broadcast_to(jnp.sum(field, axis=1, keepdims=True), (C, 128))
        spread = jnp.dot(
            group_ref[...], sums, precision=lax.Precision.HIGHEST, preferred_element_type=F32
        )
        return spread[:, :1] * (1.0 / (3 * CELLS))

    def norm(i):
        start = lat_ref[i].astype(F32) + jnp.sum(
            jnp.where(moment == step_ref[i], time_ref[...], 0.0), axis=1, keepdims=True
        )
        centred = start - group_mean(start)
        scale = lax.rsqrt(group_mean(centred * centred) + EPSILON)
        value = centred * scale
        pre = value * gain + bias
        sig = 1.0 / (1.0 + jnp.exp(-pre))
        normed[i] = value
        slope[i] = sig * (1.0 + pre * (1.0 - sig)) * gain
        rstd[i] = jnp.broadcast_to(scale, (C, 128))
        fold[...] = (pre * sig).astype(BF16).astype(F32)

    def unfold(i):
        act = fold[...]
        for at, (dy, dz) in enumerate(SHIFTS):
            move = 16 * dy + dz
            value = act
            if move != 0:
                value = jnp.where(
                    inside(lane, dy, dz), pltpu.roll(act, (-move) % CELLS, 1), 0.0
                )
            cols[i, at * C : (at + 1) * C, :] = value.astype(BF16)
        cols[i, SPAN:WIDE, :] = jnp.zeros((WIDE - SPAN, CELLS), BF16)

    for name in ("lat", "time", "group"):
        inputs[name].wait()
    norm(0)
    unfold(0)
    ag_copies["swap"].wait_recv()
    pass_on("next", nbr, shard(1))
    pass_on("previous", nbr, shard(7))
    ag_copies[2].wait_recv()
    pass_on(3, shard(6), shard(1))
    ag_copies[6].wait_recv()
    pass_on(5, shard(2), shard(7))
    upward = lax.rem(z + 2 + 4 * core, RING) * 2 + x
    downward = lax.rem(z + 6 - 4 * core, RING) * 2 + x
    pass_on(4, downward, upward)
    pass_on("x2", shard(6), nbr)
    pass_on("x6", shard(2), nbr)
    norm(1)
    unfold(1)
    for k in (3, 5, 4):
        ag_copies[k].wait_recv()
        pass_on("x%d" % k, shard(RING - k), nbr)
    for name in ("main", "last", "tgt", "spread"):
        inputs[name].wait()
    for name in (1, 7, "next", "previous", "x2", "x6", "x3", "x5", "x4"):
        ag_copies[name].wait_recv()
    for copy in ag_copies.values():
        copy.wait_send()

    main = got[:, :, :WIDE].reshape(512, WIDE)
    tails = jnp.concatenate([unpack_last(got[s, :, WIDE:]) for s in range(16)], axis=0)
    kernels = jnp.dot(main_ref[...], main, preferred_element_type=F32) + jnp.dot(
        last_ref[...], tails, preferred_element_type=F32
    )
    both[...] = kernels.astype(BF16).reshape(2, 288, WIDE)

    first, second = count_ref[0, 0], count_ref[0, 1]
    which = []
    grads = []
    zero = jnp.zeros((C, PLANE), F32)
    for i in range(2):
        place = f * 2 + i
        in_first = place < first
        in_second = (place >= first) & (place < first + second)
        which.append(in_second.astype(jnp.int32))
        live = jnp.where(in_first | in_second, reward_ref[i], 0.0)
        taps = jnp.dot(both[which[i]], cols[i], preferred_element_type=F32)
        mixed = (
            jnp.concatenate([zero, taps[:C, :-PLANE]], axis=1)
            + taps[C : 2 * C]
            + jnp.concatenate([taps[2 * C :, PLANE:], zero], axis=1)
        )
        upstream = live * (lat_ref[i].astype(F32) + mixed - tgt_ref[i].astype(F32))
        ups[i] = upstream
        rounded = upstream.astype(BF16)
        none = jnp.zeros((C, PLANE), BF16)
        ucat[i, :C] = jnp.concatenate([rounded[:, PLANE:], none], axis=1)
        ucat[i, C : 2 * C] = rounded
        ucat[i, 2 * C :] = jnp.concatenate([none, rounded[:, :-PLANE]], axis=1)
        grad = lax.dot_general(
            ucat[i], cols[i], (((1,), (1,)), ((), ())), preferred_element_type=F32
        )
        grads.append(
            (
                grad * (jnp.where(in_first, 1.0, 0.0) / CELLS),
                grad * (jnp.where(in_second, 1.0, 0.0) / CELLS),
            )
        )
    sums = jnp.concatenate(
        [(grads[0][j] + grads[1][j]).astype(BF16) for j in range(2)], axis=0
    )

    rs_copies = {}

    def send(name, src, at, to):
        copy = rcopy(src, landed.at[at], (rs_s, rs_r), at, {"fsdp": to})
        copy.start()
        rs_copies[name] = (copy, at)

    def arrived(name):
        copy, at = rs_copies[name]
        copy.wait_recv()
        return landed[at].astype(F32)

    def send_sum(name, k, column, terms, slot, at, to):
        value = part[2 * k + column].astype(F32)
        for term in terms:
            value = value + term
        stage[slot] = value.astype(BF16)
        send(name, stage.at[slot], at, to)

    for step in (4, 2, 6, 0):
        at = pl.multiple_of((z + step) * 80, 16)
        spread = jnp.dot(spread_ref[pl.ds(at, 160), :], sums, preferred_element_type=F32)
        for i in range(2):
            k = step + i
            for c in range(2):
                row = i * 80 + c * 40
                part[k * 2 + c] = pack(spread[row : row + 40])
            if 2 <= k <= 6:
                send("x%d" % k, part.at[k * 2 + 1 - x], k, nbr)
            elif k == 1:
                send("side1", part.at[k * 2 + 1 - x], 7, shard(1))
                send("own1", part.at[k * 2 + x], 8, shard(1))
            elif k == 7:
                send("side7", part.at[k * 2 + 1 - x], 9, shard(7))
                send("own7", part.at[k * 2 + x], 10, shard(7))

    def back(i):
        products = lax.dot_general(
            both[which[i]], ucat[i], (((0,), (0,)), ((), ())), preferred_element_type=F32
        )
        acc = products[4 * C : 5 * C]
        for at, (dy, dz) in enumerate(SHIFTS):
            move = 16 * dy + dz
            if move != 0:
                piece = products[at * C : (at + 1) * C]
                acc = acc + jnp.where(
                    inside(lane, -dy, -dz), pltpu.roll(piece, move % CELLS, 1), 0.0
                )
        fold[...] = acc

    results = []

    def finish(i):
        value = normed[i]
        flow = fold[...] * slope[i]
        start = rstd[i][:, :1] * (flow - group_mean(flow) - value * group_mean(flow * value))
        gi_ref[i] = (ups[i] + start).astype(BF16)
        result = pltpu.make_async_copy(gi_ref.at[i], gi_hbm.at[i], in_s.at[14 + i])
        result.start()
        results.append(result)

    back(0)
    send_sum("far4", 4, x, [arrived("x4")], 0, 11, upward)
    send_sum("far5", 5, x, [arrived("x5")], 1, 12, shard(7))
    send_sum("far3", 3, x, [arrived("x3")], 2, 13, shard(1))
    finish(0)
    send_sum("x0", 0, 1 - x, [arrived("side1"), arrived("side7")], 3, 0, nbr)
    back(1)
    far4 = arrived("far4")
    send_sum(
        "own2", 2, x,
        [arrived("x2"), arrived("far3"), jnp.where(core == 0, far4, 0.0)], 4, 14, shard(2),
    )
    send_sum(
        "own6", 6, x,
        [arrived("x6"), arrived("far5"), jnp.where(core == 1, far4, 0.0)], 5, 1, shard(6),
    )
    finish(1)
    lane_sum = part[x].astype(F32)
    for name in ("own1", "own7", "x0", "own2", "own6"):
        lane_sum = lane_sum + arrived(name)
    lane_sum = lane_sum.astype(BF16)
    lane_out[...] = jnp.concatenate(
        [lane_sum[:, :WIDE], unpack_last(lane_sum[:, WIDE:])], axis=0
    )

    dp = (dp_s, dp_r)
    own_half = OUT_TILES // 2
    share = own_half // chips
    first_tile = core * own_half
    pair = rcopy(lane_out, lane_in, dp, 30, {"dp": twin})
    pair.start()
    wide = jnp.dot(choose_out[...], lane_out[...], preferred_element_type=F32)
    told.wait_recv()
    pair.wait_recv()
    wide = wide + jnp.dot(choose_in[...], lane_in[...], preferred_element_type=F32)
    wide = wide.astype(BF16)
    for r in range(9):
        for t in range(TILES):
            table[r * TILES + t] = wide[r * 16 : (r + 1) * 16, t * 128 : (t + 1) * 128]
    table[OUT_TILES - 1] = jnp.zeros((16, 128), BF16)

    scatters = []
    for i, peer in enumerate(peers):
        copy = rcopy(
            table.at[pl.ds(first_tile + peer * share, share)], chunk_in.at[i], dp, i,
            {"dp": peer * 2 + core},
        )
        copy.start()
        scatters.append(copy)
    own = pl.ds(first_tile + chip * share, share)
    acc = table[own].astype(F32)
    for i, copy in enumerate(scatters):
        copy.wait_recv()
        acc = acc + chunk_in[i].astype(F32)
    full[own] = acc.astype(BF16)
    gathers = []
    for i, peer in enumerate(peers):
        copy = rcopy(full.at[own], full.at[own], dp, 15 + i, {"dp": peer * 2 + core})
        copy.start()
        gathers.append(copy)
    for copy in gathers:
        copy.wait_recv()
    mine = pl.ds(first_tile, own_half)
    last = rcopy(full.at[mine], full.at[mine], dp, 31, {"dp": twin})
    last.start()
    last.wait_recv()
    for copy in results:
        copy.wait()
    for copy in [copy for copy, _ in rs_copies.values()] + [pair, told, last] + scatters + gathers:
        copy.wait_send()


def finish_kernel(full_hbm, gi_in, gw_hbm, gi_out, full, gi_ref, gw_ref, sem):
    moves = [
        pltpu.make_async_copy(full_hbm, full, sem.at[0]),
        pltpu.make_async_copy(gi_in, gi_ref, sem.at[1]),
    ]
    for move in moves:
        move.start()
    for move in moves:
        move.wait()
    moves = [pltpu.make_async_copy(gi_ref, gi_out, sem.at[2])]
    moves[0].start()
    for r in range(6):
        for dx in range(3):
            at = dx * 6 + r
            line = jnp.concatenate(
                [full[at // 2 * TILES + t].astype(F32)[at % 2 * 8 :][:8] for t in range(TILES)],
                axis=1,
            )
            gw_ref[r, :, dx * SPAN : (dx + 1) * SPAN] = line[:, :SPAN]
        move = pltpu.make_async_copy(gw_ref.at[r], gw_hbm.at[r], sem.at[3 + r])
        move.start()
        moves.append(move)
    for move in moves:
        move.wait()


def local(
    chips,
    latents,
    targets,
    rewards,
    time_steps,
    time_table,
    norm_gain,
    norm_bias,
    expert_weights,
    lane_experts,
    lane_counts,
):
    main, last, spread, group = constants()
    vmem = pl.BlockSpec(memory_space=pltpu.VMEM)
    smem = pltpu.MemorySpace.SMEM
    sems = pltpu.SemaphoreType.DMA
    hbm = pl.BlockSpec(memory_space=pltpu.MemorySpace.HBM)
    full, grad_input = pl.pallas_call(
        functools.partial(kernel, chips),
        out_shape=(
            jax.ShapeDtypeStruct((OUT_TILES, 16, 128), BF16),
            jax.ShapeDtypeStruct((2, C, CELLS), BF16),
        ),
        in_specs=[hbm] * 14,
        out_specs=(vmem, hbm),
        scratch_shapes=[
            smem((2,), F32),
            smem((2,), jnp.int32),
            pltpu.VMEM((1, C), F32),
            pltpu.VMEM((1, C), F32),
            smem((1, 2), jnp.int32),
            smem((1, 2), jnp.int32),
            pltpu.VMEM((2, C, CELLS), BF16),
            pltpu.VMEM((48, 3 * SPAN), BF16),
            pltpu.VMEM((2, C, CELLS), BF16),
            pltpu.VMEM((2, C, CELLS), BF16),
            pltpu.VMEM(time_table.shape[::-1], F32),
            pltpu.VMEM(main.shape, BF16),
            pltpu.VMEM(last.shape, BF16),
            pltpu.VMEM(spread.shape, BF16),
            pltpu.VMEM(group.shape, F32),
            pltpu.VMEM((16,) + PACK, BF16),
            pltpu.VMEM((2, C, CELLS), F32),
            pltpu.VMEM((2, C, CELLS), F32),
            pltpu.VMEM((2, C, 128), F32),
            pltpu.VMEM((2, WIDE, CELLS), BF16),
            pltpu.VMEM((2, 288, WIDE), BF16),
            pltpu.VMEM((2, C, CELLS), F32),
            pltpu.VMEM((2, 288, CELLS), BF16),
            pltpu.VMEM((C, CELLS), F32),
            pltpu.VMEM((16,) + PACK, BF16),
            pltpu.VMEM((15,) + PACK, BF16),
            pltpu.VMEM((6,) + PACK, BF16),
            pltpu.VMEM((144, BLOCK), BF16),
            pltpu.VMEM((144, BLOCK), BF16),
            pltpu.VMEM((BLOCK, WIDE), BF16),
            pltpu.VMEM((BLOCK, WIDE), BF16),
            pltpu.VMEM((OUT_TILES, 16, 128), BF16),
            pltpu.VMEM((15, OUT_TILES // 2 // chips, 16, 128), BF16),
            sems((15,)),
            sems((15,)),
            sems((15,)),
            sems((15,)),
            sems((33,)),
            sems((33,)),
            sems((16,)),
        ],
        compiler_params=pltpu.CompilerParams(
            collective_id=0, has_side_effects=True, vmem_limit_bytes=60 * 2**20
        ),
    )(
        latents, targets, rewards, time_steps, time_table.T, norm_gain[None, :],
        norm_bias[None, :], expert_weights.swapaxes(0, 1).reshape(48, 3 * SPAN), lane_experts,
        lane_counts,
        jnp.asarray(main, BF16), jnp.asarray(last, BF16), jnp.asarray(spread, BF16),
        jnp.asarray(group, F32),
    )
    grad_weight, grad_input = pl.pallas_call(
        finish_kernel,
        out_shape=(
            jax.ShapeDtypeStruct((6, 8, 3 * SPAN), F32),
            jax.ShapeDtypeStruct((2, C, CELLS), BF16),
        ),
        in_specs=[hbm, hbm],
        out_specs=(hbm, hbm),
        scratch_shapes=[
            pltpu.VMEM((OUT_TILES, 16, 128), BF16),
            pltpu.VMEM((2, C, CELLS), BF16),
            pltpu.VMEM((6, 8, 3 * SPAN), F32),
            sems((9,)),
        ],
    )(full, grad_input)
    return grad_weight.swapaxes(0, 1), grad_input


def solution(mesh):
    placed = (
        P(("dp", "fsdp"), None, None),
        P(("dp", "fsdp"), None, None),
        P(("dp", "fsdp")),
        P(("dp", "fsdp")),
        P(),
        P(),
        P(),
        P(None, "fsdp", None),
        P("dp", None),
        P("dp", None),
    )
    return jax.shard_map(
        functools.partial(local, mesh.shape["dp"] // 2),
        mesh=mesh,
        in_specs=placed,
        out_specs=(P(None, "fsdp", None), P(("dp", "fsdp"), None, None)),
        check_vma=False,
    )
```
